256 devices in a mesh: dp: 4 (over y_hi, core), tm: 32 (over x, z), height: 2 (over y_lo).
Axes of the slice: x: 4, y: 4 (y_hi: 2, y_lo: 2; y = y_hi * 2 + y_lo), z: 8, core: 2. Of those that a mesh axis runs over, the one named last changes fastest.
Arguments:
- field: bfloat16 [4, 128, 18, 64, 640], P('dp', 'tm', 'height'), may hold values from -128 to 128, as said below
- cotangent: bfloat16 [4, 128, 18, 64, 640], P('dp', 'tm', 'height'), may hold values from -128 to 128, as said below
- gamma: float32 [640], replicated, may hold values from 0.1 to 1.9
- beta: float32 [640], replicated, may hold values from -2.5 to 2.5
- kernel: bfloat16 [3, 640, 640], replicated, may hold values from -0.125 to 0.125
Outputs:
- field_grad: bfloat16 [4, 128, 18, 64, 640], P('dp', 'tm', 'height')
- kernel_grad: float32 [1920, 640], P(('tm', 'height'), 'dp')
- channel_grads: float32 [3, 640], replicated
The draws below stay inside these ranges and needn't reach their ends.
Inputs may be any that keep to these rules, and one draw needn't show every extreme that they name: `field`: activations of varying scale. `cotangent`: gradients of varying scale.
All inputs are finite; a program needn't handle non-finite values.
Results may differ from the reference program's by a relative error of at most 0.0045.
Values may be sent and summed in bfloat16 or wider, within the bound.
No kernel may reach another device: no remote copies, remote signals or barrier semaphores. Data moves between devices by JAX's collectives and lax.ppermute only.
A program may use at most 128 MiB of HBM per device.

```python
import math
import jax
import jax.numpy as jnp
from jax import lax

C = 640
GROUPS = 32
CPG = 20
WCELLS = 64
FRAMES = 128
ROWS = 18
CLIPS = 4


def frame_polys():
    position = (jnp.arange(FRAMES, dtype=jnp.float32) + 0.5) / FRAMES
    first = 2.0 * position - 1.0
    second = 1.5 * first * first - 0.5
    return (first.reshape(1, FRAMES, 1, 1, 1), second.reshape(1, FRAMES, 1, 1, 1))


def frame_profile(key):
    tilt_key, sign_key, bend_key = jax.random.split(key, 3)
    first, second = frame_polys()
    tilt = jax.random.uniform(tilt_key, (CLIPS, 1, 1, 1, 1), jnp.float32, 0.55, 0.9)
    flip = (2 * jax.random.randint(sign_key, (CLIPS, 1, 1, 1, 1), 0, 2) - 1).astype(jnp.float32)
    bend = jax.random.uniform(bend_key, (CLIPS, 1, 1, 1, 1), jnp.float32, -0.6, 0.6)
    return jnp.exp(flip * tilt * first + bend * second)


def frame_offsets(key, size):
    first, second = frame_polys()
    coefs = jax.random.uniform(key, (3, CLIPS, 1, 1, 1, C), jnp.float32, -size, size)
    return coefs[0] + coefs[1] * first + coefs[2] * second


def rough_field(key, noise, low_scale, high_scale, size):
    chan_key, shape_key, offset_key = jax.random.split(key, 3)
    chan_scale = jnp.exp(jax.random.uniform(chan_key, (C,), jnp.float32, math.log(low_scale), math.log(high_scale)))
    return noise * chan_scale * frame_profile(shape_key) + frame_offsets(offset_key, size)


def draw_field(key, part):
    key = jax.random.fold_in(key, 1)
    noise_key, rest_key = jax.random.split(key)
    shape = (CLIPS, FRAMES, ROWS, WCELLS, C)
    noise = jnp.clip(jax.random.normal(noise_key, shape, jnp.float32), -5.0, 5.0)
    values = rough_field(rest_key, noise, 0.3, 1.0, 0.5)
    return values.astype(jnp.bfloat16)


def draw_cotangent(key, part):
    key = jax.random.fold_in(key, 2)
    noise_key, rest_key = jax.random.split(key)
    shape = (CLIPS, FRAMES, ROWS, WCELLS, C)
    noise = jnp.clip(jax.random.normal(noise_key, shape, jnp.float32), -5.0, 5.0)
    values = rough_field(rest_key, noise, 0.5, 1.5, 1.2)
    return values.astype(jnp.bfloat16)


def scatter_about(key, extent, spread, reach, held_as=jnp.bfloat16):
    values = jax.random.normal(key, extent, jnp.float32) * spread
    return jnp.minimum(jnp.maximum(values, -reach), reach).astype(held_as)


def setup_inputs(seed: int = 0) -> dict:
    arg_keys = jax.random.split(jax.random.key(seed), 6)
    field = draw_field(jax.random.fold_in(arg_keys[5], 71), 0)
    cotangent = draw_cotangent(jax.random.fold_in(arg_keys[5], 71), 0)
    gamma = jnp.clip(1.0 + 0.18 * jax.random.normal(arg_keys[2], (C,), jnp.float32), 0.1, 1.9)
    beta = scatter_about(arg_keys[3], (C,), 0.5, 2.5, jnp.float32)
    kernel = scatter_about(arg_keys[4], (3, C, C), (3 * C) ** -0.5, 0.125)
    return {"field": field, "cotangent": cotangent, "gamma": gamma, "beta": beta, "kernel": kernel}


def flatten(array):
    return array.reshape(-1, C)

def one_clip(pair):
    field_clip, cot_clip, gamma, beta, kernel = pair
    chan_total = FRAMES * ROWS * WCELLS * CPG
    field_wide = field_clip.astype(jnp.float32)
    group_mean = field_wide.sum((0, 1, 2)).reshape(GROUPS, CPG).sum(1) / chan_total
    centered = field_wide - jnp.repeat(group_mean, CPG)
    group_var = (centered * centered).sum((0, 1, 2)).reshape(GROUPS, CPG).sum(1) / chan_total
    inv_spread = jnp.repeat(lax.rsqrt(group_var + 1e-05), CPG)
    unit_norm = centered * inv_spread
    normed = unit_norm * gamma + beta
    sigmoid_val = jax.nn.sigmoid(normed)
    activated = (normed * sigmoid_val).astype(jnp.bfloat16)
    padded = jnp.pad(cot_clip, ((1, 1), (0, 0), (0, 0), (0, 0)))
    grad_act = jnp.zeros((FRAMES * ROWS * WCELLS, C), jnp.float32)
    taps = []
    for offset in range(3):
        window = flatten(padded[2 - offset:2 - offset + FRAMES])
        grad_act = grad_act + lax.dot_general(window, kernel[offset], (((1,), (1,)), ((), ())), preferred_element_type=jnp.float32)
        taps.append(lax.dot_general(flatten(activated), window, (((0,), (0,)), ((), ())), preferred_element_type=jnp.float32))
    grad_act = grad_act.reshape(field_clip.shape)
    grad_normed = grad_act * sigmoid_val * (1.0 + normed * (1.0 - sigmoid_val))
    s_beta = grad_normed.sum((0, 1, 2))
    s_gamma = (grad_normed * unit_norm).sum((0, 1, 2))
    s_bias = cot_clip.astype(jnp.float32).sum((0, 1, 2))
    mean_first = jnp.repeat((gamma * s_beta).reshape(GROUPS, CPG).sum(1) / chan_total, CPG)
    mean_second = jnp.repeat((gamma * s_gamma).reshape(GROUPS, CPG).sum(1) / chan_total, CPG)
    field_grad = cot_clip.astype(jnp.float32) + inv_spread * (gamma * grad_normed - mean_first - unit_norm * mean_second)
    tap_grad = jnp.stack(taps).reshape(3 * C, C)
    return (field_grad.astype(jnp.bfloat16), tap_grad, jnp.stack([s_beta, s_gamma, s_bias]))

def reference(field, cotangent, gamma, beta, kernel):
    loss_scale = 1.0 / math.sqrt(CLIPS * FRAMES * ROWS * WCELLS)
    field_grad, tap_grads, chan_sums = lax.map(lambda pair: one_clip((pair[0], pair[1], gamma, beta, kernel)), (field, cotangent))
    return (field_grad, tap_grads.sum(0) * loss_scale, chan_sums.sum(0) * loss_scale)
```

```python
import math

import jax
import jax.numpy as jnp
from jax import lax
from jax.sharding import PartitionSpec as P

GROUPS = 32
AXES = ("dp", "tm", "height")
BIT = {"yh": 7, "core": 6, "x1": 5, "x0": 4, "z2": 3, "z1": 2, "z0": 1, "yl": 0}


def swap(value, bit):
    mask = 1 << BIT[bit]
    return lax.ppermute(value, AXES, [(i, i ^ mask) for i in range(256)])


def with_halo(array):
    count = lax.axis_size("tm")
    up = [(i, i + 1) for i in range(count - 1)]
    down = [(j, i) for i, j in up]
    before = lax.ppermute(array[:, -1:], "tm", up)
    after = lax.ppermute(array[:, :1], "tm", down)
    return jnp.concatenate([before, array, after], axis=1)


def halve(total, axis, bit, own, wire):
    keep = lax.dynamic_index_in_dim(total, own[bit], axis, keepdims=False)
    send = lax.dynamic_index_in_dim(total, 1 - own[bit], axis, keepdims=False)
    return keep + swap(send.astype(wire), bit).astype(jnp.float32)


def per_device(field, cotangent, gamma, beta, kernel):
    _, frames, rows, cells, width = field.shape
    per_group = width // GROUPS
    count = rows * frames * cells * per_group
    chan_total = count * lax.axis_size("tm") * lax.axis_size("height")
    loss_scale = 1.0 / math.sqrt(4 * 128 * 18 * 64)
    place = lax.axis_index(AXES)
    own = {name: (place >> bit) & 1 for name, bit in BIT.items()}

    def to_groups(values):
        return values.reshape(GROUPS, per_group).sum(1)

    def to_channels(values):
        return jnp.repeat(values, per_group)

    padded = with_halo(cotangent)
    field_wide = field.astype(jnp.float32)
    mean = to_groups(field_wide.sum((0, 1, 2, 3))) / count
    centered = field_wide - to_channels(mean)
    second = to_groups((centered * centered).sum((0, 1, 2, 3)))
    stats = jnp.stack([mean, second])
    size = float(count)
    for bit in ("z0", "x0", "yl", "z1", "x1", "z2"):
        other = swap(stats, bit)
        gap = stats[0] - other[0]
        stats = jnp.stack(
            [0.5 * (stats[0] + other[0]), stats[1] + other[1] + gap * gap * (0.5 * size)]
        )
        size = 2.0 * size
    group_mean = to_channels(stats[0])
    inv_spread = to_channels(lax.rsqrt(stats[1] / chan_total + 1e-05))
    unit_norm = (field_wide - group_mean) * inv_spread
    normed = unit_norm * gamma + beta
    sigmoid_val = jax.nn.sigmoid(normed)
    activated = (normed * sigmoid_val).astype(jnp.bfloat16)
    act_rows = activated.reshape(-1, width)
    grad_act = jnp.zeros(act_rows.shape, jnp.float32)
    taps = []
    for offset in range(3):
        window = padded[:, 2 - offset : 2 - offset + frames].reshape(-1, width)
        grad_act = grad_act + lax.dot_general(
            window, kernel[offset], (((1,), (1,)), ((), ())), preferred_element_type=jnp.float32
        )
        taps.append(
            lax.dot_general(
                act_rows, window, (((0,), (0,)), ((), ())), preferred_element_type=jnp.float32
            )
        )
    tap = jnp.stack(taps).reshape(64, 30, 2, 2, 160).transpose(3, 0, 1, 2, 4)
    tap = jnp.pad(tap, ((0, 0), (0, 0), (0, 2), (0, 0), (0, 0)))
    tap = tap.reshape(2, 2, 2, 2, 2, 2, 2, 32, 320)
    tap = halve(tap, 0, "core", own, jnp.bfloat16)
    tap = halve(tap, 4, "z0", own, jnp.bfloat16)
    tap = halve(tap, 1, "x0", own, jnp.bfloat16)
    tap = halve(tap, 3, "yl", own, jnp.bfloat16)
    tap = halve(tap, 2, "z1", own, jnp.float32)
    tap = halve(tap, 0, "x1", own, jnp.float32)
    tap = halve(tap, 0, "z2", own, jnp.float32)
    tap = halve(tap.reshape(32, 2, 160), 1, "yh", own, jnp.float32)
    kernel_grad = tap[:30] * loss_scale

    grad_act = grad_act.reshape(field.shape)
    grad_normed = grad_act * sigmoid_val * (1.0 + normed * (1.0 - sigmoid_val))
    cot_wide = cotangent.astype(jnp.float32)
    sums = jnp.stack(
        [
            grad_normed.sum((0, 1, 2, 3)),
            (grad_normed * unit_norm).sum((0, 1, 2, 3)),
            cot_wide.sum((0, 1, 2, 3)),
        ]
    )
    for bit in ("z0", "x0", "yl", "z1", "x1", "z2"):
        sums = sums + swap(sums, bit)
    mean_first = to_channels(to_groups(gamma * sums[0]) / chan_total)
    mean_second = to_channels(to_groups(gamma * sums[1]) / chan_total)
    field_grad = (
        cot_wide + inv_spread * (gamma * grad_normed - mean_first - unit_norm * mean_second)
    ).astype(jnp.bfloat16)
    for bit in ("core", "yh"):
        sums = sums + swap(sums, bit)
    return (field_grad, kernel_grad, sums * loss_scale)


def solution(mesh):
    spread = P("dp", "tm", "height", None, None)
    return jax.shard_map(
        per_device,
        mesh=mesh,
        in_specs=(spread, spread, P(), P(), P()),
        out_specs=(spread, P(("tm", "height"), "dp"), P()),
        check_vma=False,
    )
```

```python
import math

import jax
import jax.numpy as jnp
import ml_dtypes
import numpy as np
from jax import lax
from jax.experimental import pallas as pl
from jax.experimental.pallas import tpu as pltpu
from jax.sharding import PartitionSpec as P

GROUPS = 32
FRAME = 576
AXES = ("dp", "tm", "height")
BIT = {"yh": 7, "core": 6, "x1": 5, "x0": 4, "z2": 3, "z1": 2, "z0": 1, "yl": 0}
OWNER = ("x1", "x0", "z2", "z1", "z0", "yl")
ORDER_A = ("z0", "x0", "yl", "x1", "z2", "z1")
ORDER_B = ("yl", "z0", "x0", "x1", "z2", "z1")
f32 = jnp.float32
bf16 = jnp.bfloat16
IN_VMEM = pl.BlockSpec(memory_space=pltpu.VMEM)
IN_SMEM = pl.BlockSpec(memory_space=pltpu.SMEM)


def params(mib):
    return pltpu.CompilerParams(vmem_limit_bytes=mib * 2**20)


def cost(flops, moved, transcendentals=0):
    return pl.CostEstimate(flops=flops, bytes_accessed=moved, transcendentals=transcendentals)


def pairs(bit):
    mask = 1 << BIT[bit]
    return [(i, i ^ mask) for i in range(256)]


def neighbours(axis):
    out = []
    for i in range(256):
        bit = {name: (i >> at) & 1 for name, at in BIT.items()}
        x, y = 2 * bit["x1"] + bit["x0"], 2 * bit["yh"] + bit["yl"]
        z = 4 * bit["z2"] + 2 * bit["z1"] + bit["z0"]
        place = {"x": x, "y": y, "z": z}
        size = 8 if axis == "z" else 4
        at = place[axis]
        step = 1 if (at % 2 == 0) == (bit["core"] == 0) else -1
        place[axis] = (at + step) % size
        x, y, z = place["x"], place["y"], place["z"]
        out.append((i, (((y >> 1) * 2 + bit["core"]) * 32 + x * 8 + z) * 2 + (y & 1)))
    return out


NEAR = {"z0": "z", "x0": "x", "yl": "y"}


def swap(value, bit):
    return lax.ppermute(value, AXES, pairs(bit))


def near_halve(total, bit, own):
    halves = total.reshape((2, total.shape[0] // 2) + total.shape[1:])
    keep = lax.dynamic_index_in_dim(halves, own[bit], 0, keepdims=False)
    send = lax.dynamic_index_in_dim(halves, 1 - own[bit], 0, keepdims=False)
    got = lax.ppermute(send.astype(bf16), AXES, neighbours(NEAR[bit]))
    return keep + got.astype(f32)


def far_swap(send, sums, bit):
    high = lax.reduce_precision(sums, 8, 7)
    rest = sums - high
    middle = lax.reduce_precision(rest, 8, 7)
    parts = [part.astype(bf16) for part in (high, middle, rest - middle)]
    rows = send.reshape(-1, 128)
    got = swap(jnp.concatenate([rows.astype(bf16)] + parts, axis=0), bit).astype(f32)
    cut, count = rows.shape[0], sums.shape[0]
    other = [got[cut + i * count : cut + (i + 1) * count] for i in range(3)]
    return got[:cut].reshape(send.shape), sums + (other[0] + (other[1] + other[2]))


def far_halve(total, axis, bit, own, sums):
    keep = lax.dynamic_index_in_dim(total, own[bit], axis, keepdims=False)
    send = lax.dynamic_index_in_dim(total, 1 - own[bit], axis, keepdims=False)
    got, sums = far_swap(send, sums, bit)
    return keep + got, sums


def stats_kernel(field_ref, out_ref):
    count = field_ref.shape[0]
    mean = jnp.sum(field_ref[...].astype(f32), axis=0, keepdims=True) * (1.0 / count)
    gap = field_ref[...].astype(f32) - mean
    second = jnp.sum(gap * gap, axis=0, keepdims=True)
    out_ref[0] = jnp.concatenate([mean, second, jnp.zeros((6, mean.shape[1]), f32)], axis=0)


def frame_stats(field):
    rows, width = field.shape
    frames = rows // FRAME
    return pl.pallas_call(
        stats_kernel,
        grid=(frames,),
        in_specs=[pl.BlockSpec((FRAME, width), lambda i: (i, 0))],
        out_specs=pl.BlockSpec((1, 8, width), lambda i: (i, 0, 0)),
        out_shape=jax.ShapeDtypeStruct((frames, 8, width), f32),
        compiler_params=params(16),
        cost_estimate=cost(rows * width * 4, rows * width * 2),
    )(field)


def sigmoid(values):
    return 0.5 * jnp.tanh(0.5 * values) + 0.5


def packed_places(order):
    out = []
    for block in range(64):
        bit = {name: (block >> (5 - i)) & 1 for i, name in enumerate(OWNER)}
        place = 0
        for name in order:
            place = 2 * place + bit[name]
        out.append(place)
    return out


def taps_a_kernel(core_ref, field_ref, coef_ref, cot_ref, act_ref, send_ref, keep_ref, acc, wide):
    core = core_ref[0]
    width, rows = field_ref.shape
    for q in range(3):
        wide[q] = jnp.broadcast_to(coef_ref[:, q : q + 1], (width, 128))

    def activate(j):
        for at in (256 * j, 256 * j + 128):
            lanes = slice(at, at + 128)
            normed = (field_ref[:, lanes].astype(f32) - wide[0]) * wide[1] + wide[2]
            act_ref[:, lanes] = (normed * sigmoid(normed)).astype(bf16)

    activate(0)
    for j in range(rows // 256):
        if 256 * (j + 1) < rows:
            activate(j + 1)
        act = act_ref[:, 256 * j : 256 * j + 256]
        for k in range(3):
            start = FRAME * (2 - k) + 256 * j
            part = jnp.dot(act, cot_ref[start : start + 256, :], preferred_element_type=f32)
            if j == 0:
                acc[width * k : width * k + width, :] = part
            else:
                acc[width * k : width * k + width, :] += part
    acc[3 * width :, :] = jnp.zeros((8, acc.shape[1]), f32)
    mine = pl.ds(pl.multiple_of(core * 128, 128), 128)
    other = pl.ds(pl.multiple_of((1 - core) * 128, 128), 128)
    for block, place in enumerate(packed_places(ORDER_A)):
        keep_ref[place] = acc[30 * block : 30 * block + 32, mine]
        send_ref[place] = acc[30 * block : 30 * block + 32, other].astype(bf16)


def taps_a(core, field_t, coef, cot):
    width, rows = field_t.shape
    lanes = cot.shape[1]
    return pl.pallas_call(
        taps_a_kernel,
        in_specs=[IN_SMEM, IN_VMEM, IN_VMEM, IN_VMEM],
        out_specs=[IN_VMEM] * 3,
        out_shape=[
            jax.ShapeDtypeStruct((width, rows), bf16),
            jax.ShapeDtypeStruct((64, 32, 128), bf16),
            jax.ShapeDtypeStruct((64, 32, 128), f32),
        ],
        scratch_shapes=[
            pltpu.VMEM((3 * width + 8, lanes), f32),
            pltpu.VMEM((3, width, 128), f32),
        ],
        compiler_params=params(40),
        cost_estimate=cost(6 * width * rows * lanes, 10**7, width * rows),
    )(core, field_t, coef, cot)


def taps_b_kernel(core_ref, act_ref, cot_ref, send_ref, keep_ref, acc):
    core = core_ref[0]
    width, rows = act_ref.shape
    for k in range(3):
        start = FRAME * (2 - k)
        acc[width * k : width * k + width, :] = jnp.dot(
            act_ref[...], cot_ref[start : start + rows, :], preferred_element_type=f32
        )
    acc[3 * width :, :] = jnp.zeros((8, acc.shape[1]), f32)
    mine = pl.ds(pl.multiple_of(core * 128, 128), 128)
    other = pl.ds(pl.multiple_of((1 - core) * 128, 128), 128)
    low = lax.broadcasted_iota(jnp.int32, (16, 128), 1) < 64
    first = core == 0
    for block, place in enumerate(packed_places(ORDER_B)):
        at = 30 * block
        keep_ref[place, 0:32] = acc[at : at + 32, mine]
        send_ref[place, 0:32] = acc[at : at + 32, other].astype(bf16)
        top, bottom = acc[at : at + 16, 256:384], acc[at + 16 : at + 32, 256:384]
        zero = jnp.where(low, top, pltpu.roll(bottom, 64, 1))
        one = jnp.where(low, pltpu.roll(top, 64, 1), bottom)
        keep_ref[place, 32:48] = jnp.where(first, zero, one)
        send_ref[place, 32:48] = jnp.where(first, one, zero).astype(bf16)


def taps_b(core, act, cot):
    width, rows = act.shape
    lanes = cot.shape[1]
    return pl.pallas_call(
        taps_b_kernel,
        in_specs=[IN_SMEM, IN_VMEM, IN_VMEM],
        out_specs=[IN_VMEM] * 2,
        out_shape=[
            jax.ShapeDtypeStruct((64, 48, 128), bf16),
            jax.ShapeDtypeStruct((64, 48, 128), f32),
        ],
        scratch_shapes=[pltpu.VMEM((3 * width + 8, lanes), f32)],
        compiler_params=params(40),
        cost_estimate=cost(6 * width * rows * lanes, 10**7),
    )(core, act, cot)


def normed_kernel(field_ref, grad_ref, coef_ref, out_ref, sums_ref):
    mean, inv, gamma, beta = (coef_ref[q : q + 1, :] for q in range(4))
    unit = (field_ref[...].astype(f32) - mean) * inv
    normed = unit * gamma + beta
    gate = sigmoid(normed)
    grad = grad_ref[...] * gate * (1.0 + normed * (1.0 - gate))
    out_ref[...] = grad
    part = jnp.concatenate(
        [
            jnp.sum(grad, axis=0, keepdims=True),
            jnp.sum(grad * unit, axis=0, keepdims=True),
            jnp.zeros((6, grad.shape[1]), f32),
        ],
        axis=0,
    )

    @pl.when(pl.program_id(0) == 0)
    def _():
        sums_ref[...] = part

    @pl.when(pl.program_id(0) > 0)
    def _():
        sums_ref[...] += part


def grad_of_normed(field, grad_act, coef, block=288):
    rows, width = field.shape
    tile = pl.BlockSpec((block, width), lambda i: (i, 0))
    top = pl.BlockSpec((8, width), lambda i: (0, 0))
    return pl.pallas_call(
        normed_kernel,
        grid=(rows // block,),
        in_specs=[tile, tile, top],
        out_specs=[tile, top],
        out_shape=[
            jax.ShapeDtypeStruct((rows, width), f32),
            jax.ShapeDtypeStruct((8, width), f32),
        ],
        compiler_params=params(24),
        cost_estimate=cost(rows * width * 14, rows * width * 10, rows * width),
    )(field, grad_act, coef)


def result_kernel(cot_ref, grad_ref, field_ref, coef_ref, out_ref):
    mean, inv, gamma, first, second = (coef_ref[q : q + 1, :] for q in range(5))
    unit = (field_ref[...].astype(f32) - mean) * inv
    out_ref[...] = (
        cot_ref[...].astype(f32) + inv * (gamma * grad_ref[...] - first - unit * second)
    ).astype(bf16)


def grad_of_field(cot, grad, field, coef, block=288):
    rows, width = field.shape
    tile = pl.BlockSpec((block, width), lambda i: (i, 0))
    return pl.pallas_call(
        result_kernel,
        grid=(rows // block,),
        in_specs=[tile, tile, tile, pl.BlockSpec((8, width), lambda i: (0, 0))],
        out_specs=tile,
        out_shape=jax.ShapeDtypeStruct((rows, width), bf16),
        compiler_params=params(24),
        cost_estimate=cost(rows * width * 9, rows * width * 10),
    )(cot, grad, field, coef)


def column_choice():
    order = [(c, h) for c in range(2) for h in range(2)]
    spread = [(160 * (2 * h + c), part) for part in ((0, 64), (64, 128), (128, 160)) for c, h in order]
    columns = np.concatenate([np.arange(base + lo, base + hi) for base, (lo, hi) in spread])
    chosen = np.zeros((640, 640), ml_dtypes.bfloat16)
    chosen[columns, np.arange(640)] = 1
    return chosen[:, :256], chosen[:, 256:]


def per_device(field, cotangent, gamma, beta, kernel):
    _, frames, rows, cells, width = field.shape
    per_group = width // GROUPS
    chan_total = frames * rows * cells * per_group * 64
    loss_scale = 1.0 / math.sqrt(4 * 128 * 18 * 64)
    place = lax.axis_index(AXES)
    own = {name: (place >> bit) & 1 for name, bit in BIT.items()}
    core = own["core"].astype(jnp.int32).reshape(1)

    def to_channels(values):
        return jnp.repeat(values, per_group)

    cot = cotangent.reshape(-1, width)
    up = [(i, i + 1) for i in range(31)]
    down = [(j, i) for i, j in up]
    before = lax.ppermute(cot[-FRAME:], "tm", up)
    after = lax.ppermute(cot[:FRAME], "tm", down)

    flat = field.reshape(-1, width)
    local = frame_stats(flat)
    means = local[:, 0].reshape(frames, GROUPS, per_group)
    mean = means.mean((0, 2))
    gaps = means - mean[None, :, None]
    second = local[:, 1].reshape(frames, GROUPS, per_group).sum((0, 2)) + FRAME * (gaps * gaps).sum(
        (0, 2)
    )
    stats = jnp.stack([mean, second])
    size = float(frames * rows * cells * per_group)
    for bit in ("x0", "yl", "x1", "z0", "z1", "z2"):
        other = swap(stats, bit)
        gap = stats[0] - other[0]
        stats = jnp.stack(
            [0.5 * (stats[0] + other[0]), stats[1] + other[1] + gap * gap * (0.5 * size)]
        )
        size = 2.0 * size

    padded = jnp.concatenate([before, cot, after], axis=0)
    choose_a, choose_b = column_choice()
    cot_a = jnp.dot(padded, choose_a, preferred_element_type=f32).astype(bf16)
    cot_b = jnp.dot(padded, choose_b, preferred_element_type=f32).astype(bf16)
    field_t = flat.T
    span = frames * FRAME
    grad_act = sum(
        lax.dot_general(
            padded[FRAME * (2 - k) : FRAME * (2 - k) + span],
            kernel[k],
            (((1,), (1,)), ((), ())),
            preferred_element_type=f32,
        )
        for k in range(3)
    )
    bias_sum = cot.astype(f32).sum(0)

    mean_c = to_channels(stats[0])
    inv_c = to_channels(lax.rsqrt(stats[1] / chan_total + 1e-05))
    coef_t = jnp.pad(jnp.stack([mean_c, inv_c * gamma, beta], axis=1), ((0, 0), (0, 125)))
    act_t, send_a, keep_a = taps_a(core, field_t, coef_t, cot_a)
    total_a = keep_a + swap(send_a, "core").astype(f32)
    send_b, keep_b = taps_b(core, act_t, cot_b)
    total_b = keep_b + swap(send_b, "core").astype(f32)

    zeros = jnp.zeros((width,), f32)
    coef = jnp.stack([mean_c, inv_c, gamma, beta] + [zeros] * 4)
    grad_normed, sums = grad_of_normed(flat, grad_act, coef)
    total = jnp.concatenate([sums[0], sums[1], bias_sum])
    grouped = (gamma * sums[:2]).reshape(2, GROUPS, per_group).sum(2).reshape(-1)
    total = total + swap(total.reshape(15, 128), "core").reshape(-1)
    sums = jnp.concatenate([total, grouped, jnp.zeros((64,), f32)]).reshape(16, 128)

    for bit in ORDER_A[:3]:
        total_a = near_halve(total_a, bit, own)
    for bit in ORDER_B[:3]:
        total_b = near_halve(total_b, bit, own)
    for bit in ("z0", "x0", "yl"):
        sums = sums + swap(sums, bit)
    taps = jnp.concatenate([total_a, total_b], axis=1).reshape(2, 2, 2, 80, 128)
    taps, sums = far_halve(taps, 2, "z1", own, sums)
    taps, sums = far_halve(taps, 0, "x1", own, sums)
    taps, sums = far_halve(taps, 0, "z2", own, sums)
    means = sums[15, :64].reshape(2, GROUPS) / chan_total
    coef = jnp.stack(
        [mean_c, inv_c, gamma, to_channels(means[0]), to_channels(means[1])] + [zeros] * 3
    )
    field_grad = grad_of_field(cot, grad_normed, flat, coef)

    got, sums = far_swap(taps, sums, "yh")
    taps = taps + got
    rest = jnp.concatenate([taps[64:, :64], taps[64:, 64:]], axis=0)
    whole = jnp.concatenate(
        [taps[:32].reshape(32, 2, 64), taps[32:64].reshape(32, 2, 64), rest.reshape(32, 2, 32)],
        axis=2,
    )
    kernel_grad = lax.dynamic_index_in_dim(whole, own["yh"], 1, keepdims=False)[:30] * loss_scale
    channel_grads = sums[:15].reshape(3, width) * loss_scale
    return (field_grad.reshape(field.shape), kernel_grad, channel_grads)


def solution(mesh):
    spread = P("dp", "tm", "height", None, None)
    return jax.shard_map(
        per_device,
        mesh=mesh,
        in_specs=(spread, spread, P(), P(), P()),
        out_specs=(spread, P(("tm", "height"), "dp"), P()),
        check_vma=False,
    )
```

```python
import functools
import math

import jax
import jax.numpy as jnp
from jax import lax
from jax.experimental import pallas as pl
from jax.experimental.pallas import tpu as pltpu
from jax.sharding import PartitionSpec as P

GROUPS = 32
CPG = 20
FRAME = 576
CHUNK = 768
CHAN_TOTAL = 128 * 18 * 64 * CPG
AXES = ("dp", "tm", "height")
BIT = {"yh": 7, "core": 6, "x1": 5, "x0": 4, "z2": 3, "z1": 2, "z0": 1, "yl": 0}
OWNER = ("x1", "x0", "z2", "z1", "z0", "yl")
ORDERS = (("z0", "x0", "yl", "x1", "z1"), ("yl", "z0", "x0", "x1", "z1"))
f32 = jnp.float32
bf16 = jnp.bfloat16
IN_VMEM = pl.BlockSpec(memory_space=pltpu.VMEM)
ANYWHERE = pl.BlockSpec(memory_space=pl.ANY)
IN_SMEM = pl.BlockSpec(memory_space=pltpu.SMEM)


def params(mib):
    return pltpu.CompilerParams(vmem_limit_bytes=mib * 2**20)


def vmem(shape, dtype):
    return pltpu.VMEM(shape, dtype)


def in_hbm(*arrays):
    return [pltpu.with_memory_space_constraint(array, pltpu.HBM) for array in arrays]


def cost(flops, moved, transcendentals=0):
    return pl.CostEstimate(flops=flops, bytes_accessed=moved, transcendentals=transcendentals)


def pairs(bits):
    mask = sum(1 << BIT[bit] for bit in bits)
    return [(i, i ^ mask) for i in range(256)]


def neighbours(axis):
    out = []
    for i in range(256):
        bit = {name: (i >> at) & 1 for name, at in BIT.items()}
        x, y = 2 * bit["x1"] + bit["x0"], 2 * bit["yh"] + bit["yl"]
        z = 4 * bit["z2"] + 2 * bit["z1"] + bit["z0"]
        place = {"x": x, "y": y, "z": z}
        size = 8 if axis == "z" else 4
        at = place[axis]
        step = 1 if (at % 2 == 0) == (bit["core"] == 0) else -1
        place[axis] = (at + step) % size
        x, y, z = place["x"], place["y"], place["z"]
        out.append((i, (((y >> 1) * 2 + bit["core"]) * 32 + x * 8 + z) * 2 + (y & 1)))
    return out


NEAR = {"z0": "z", "x0": "x", "yl": "y"}


def swap(value, *bits):
    chosen = pairs(bits)
    if bits == ("z1",):
        both = pairs(("z1", "z2"))
        chosen = [both[i] if (i >> BIT["core"]) & 1 else pair for i, pair in enumerate(chosen)]
    return lax.ppermute(value, AXES, chosen)


def half(total, axis, index):
    return lax.dynamic_index_in_dim(total, index, axis, False, allow_negative_indices=False)


def far_swap(send, sums, bit):
    high = lax.reduce_precision(sums, 8, 7)
    rest = sums - high
    middle = lax.reduce_precision(rest, 8, 7)
    parts = [part.astype(bf16) for part in (high, middle, rest - middle)]
    rows = send.reshape(-1, 128)
    got = swap(jnp.concatenate([rows.astype(bf16)] + parts, axis=0), bit).astype(f32)
    cut, count = rows.shape[0], sums.shape[0]
    other = [got[cut + i * count : cut + (i + 1) * count] for i in range(3)]
    return got[:cut].reshape(send.shape), sums + (other[0] + (other[1] + other[2]))


def far_halve(total, axis, bit, own, off, sums):
    keep = half(total, axis, own[bit])
    send = half(total, axis, off[bit])
    got, sums = far_swap(send, sums, bit)
    return keep + got, sums


def group_rows(lanes, first):
    channel = lax.broadcasted_iota(jnp.int32, (640, lanes), 0)
    start = (lax.broadcasted_iota(jnp.int32, (640, lanes), 1) - first) * CPG
    return jnp.where((channel >= start) & (channel < start + CPG), 1.0, 0.0).astype(f32)


def group_columns(rows, first):
    channel = lax.broadcasted_iota(jnp.int32, (rows, 640), 1)
    start = (lax.broadcasted_iota(jnp.int32, (rows, 640), 0) - first) * CPG
    return jnp.where((channel >= start) & (channel < start + CPG), 1.0, 0.0).astype(f32)


def exact(left, right):
    return jnp.dot(left, right, preferred_element_type=f32, precision=lax.Precision.HIGHEST)


def stats_kernel(
    bits_ref, upper_ref, lower_ref, head_ref, tail_ref, out_ref, first_ref, final_ref, means, seconds
):
    step, last = pl.program_id(0), pl.num_programs(0) - 1
    count = upper_ref.shape[0]
    @pl.when(step == 0)
    def _():
        first_ref[...] = head_ref[...]
        final_ref[...] = tail_ref[...]
        means[...] = jnp.zeros_like(means)
        seconds[...] = jnp.zeros_like(seconds)

    for part, ref in enumerate((upper_ref, lower_ref)):
        mean = jnp.sum(ref[...].astype(f32), axis=0, keepdims=True) * (1.0 / count)
        gap = ref[...].astype(f32) - mean
        means[pl.ds(2 * step + part, 1), :] = mean
        seconds[0:1, :] += jnp.sum(gap * gap, axis=0, keepdims=True)

    @pl.when(step == last)
    def _():
        blocks = BLOCKS
        total = jnp.sum(means[...], axis=0, keepdims=True) * (1.0 / blocks)
        to_groups, to_channels = group_rows(128, 0), group_columns(128, 0)
        eight = jnp.broadcast_to(total, (8, total.shape[1]))
        mean = exact(eight, to_groups) * (1.0 / CPG)
        gaps = means[0:blocks, :] - exact(mean, to_channels)[0:1]
        spread = seconds[0:1, :] + count * jnp.sum(gaps * gaps, axis=0, keepdims=True)
        second = exact(jnp.broadcast_to(spread, eight.shape), to_groups)
        both = jnp.concatenate([mean[0:1], second[0:1]], axis=0)
        out_ref[...] = jnp.broadcast_to(both[None], out_ref.shape)


BLOCKS = 6


def local_stats(bits, field, cot):
    rows, width = field.shape
    block = rows // BLOCKS
    field = pltpu.with_memory_space_constraint(field, pltpu.HBM)
    return pl.pallas_call(
        stats_kernel,
        grid=(BLOCKS // 2,),
        in_specs=[
            IN_SMEM,
            pl.BlockSpec((block, width), lambda i: (2 * i, 0)),
            pl.BlockSpec((block, width), lambda i: (2 * i + 1, 0)),
            pl.BlockSpec((FRAME, width), lambda i: (0, 0)),
            pl.BlockSpec((FRAME, width), lambda i: (rows // FRAME - 1, 0)),
        ],
        out_specs=[
            pl.BlockSpec((64, 2, 128), lambda i: (0, 0, 0)),
            pl.BlockSpec((FRAME, width), lambda i: (0, 0)),
            pl.BlockSpec((FRAME, width), lambda i: (0, 0)),
        ],
        out_shape=[
            jax.ShapeDtypeStruct((64, 2, 128), f32),
            pltpu.HBM((FRAME, width), bf16),
            pltpu.HBM((FRAME, width), bf16),
        ],
        scratch_shapes=[
            pltpu.VMEM((8, width), f32),
            pltpu.VMEM((8, width), f32),
        ],
        compiler_params=params(16),
        cost_estimate=cost(rows * width * 4, rows * width * 2),
    )(bits, field, field, *in_hbm(cot, cot))


def turn_kernel(field_ref, turned_ref):
    turned_ref[...] = field_ref[...].T


def turned(field):
    rows, width = field.shape
    return pl.pallas_call(
        turn_kernel,
        grid=(width // 128,),
        in_specs=[pl.BlockSpec((rows, 128), lambda i: (0, i))],
        out_specs=pl.BlockSpec((128, rows), lambda i: (i, 0)),
        out_shape=pltpu.HBM((width, rows), bf16),
        compiler_params=params(12),
        cost_estimate=cost(10**9, 10**7),
    )(field)


def sigmoid(values):
    return 0.5 * jnp.tanh(0.5 * values) + 0.5


def owners(chain):
    out = []
    for block in range(64):
        bit = {name: (block >> (5 - i)) & 1 for i, name in enumerate(OWNER)}
        if bit["z2"] == chain:
            place = 0
            for name in ORDERS[chain]:
                place = 2 * place + bit[name]
            out.append((block, place))
    return out


def segments(chain):
    parts = {}
    for start in range(240 * chain, 1920, 480):
        row = start
        while row < start + 240:
            tap, channel = divmod(row, 640)
            length = min(start + 240 - row, 640 - channel)
            parts.setdefault(tap, []).append((channel, length))
            row += length
    out, at = [], 0
    for tap in sorted(parts):
        out.append((tap, tuple(parts[tap]), at))
        at += sum(length for _, length in parts[tap])
    return out


def add_taps(chain, acc, act_ref, cot_ref, j):
    lanes = slice(CHUNK * j, CHUNK * j + CHUNK)
    for tap, parts, at in segments(chain):
        start = FRAME * (2 - tap) + CHUNK * j
        rows = [act_ref[channel : channel + length, lanes] for channel, length in parts]
        rows = rows[0] if len(rows) == 1 else jnp.concatenate(rows, axis=0)
        part = jnp.dot(rows, cot_ref[start : start + CHUNK, :], preferred_element_type=f32)
        if j == 0:
            acc[at : at + rows.shape[0], :] = part
        else:
            acc[at : at + rows.shape[0], :] += part


def pack_taps(chain, first, acc, send_ref, keep_ref):
    lane = lax.broadcasted_iota(jnp.int32, (32, 128), 1)
    low = lax.broadcasted_iota(jnp.int32, (16, 128), 1)
    for number, (_, place) in enumerate(owners(chain)):
        rows = slice(30 * number, 30 * number + 32)
        tile = [acc[rows, 128 * q : 128 * q + 128] for q in range(5)]
        main = [
            tile[0],
            jnp.where(lane < 96, pltpu.roll(tile[1], 96, 1), pltpu.roll(tile[2], 96, 1)),
            jnp.where(lane < 64, pltpu.roll(tile[2], 64, 1), pltpu.roll(tile[3], 64, 1)),
            jnp.where(lane < 32, pltpu.roll(tile[3], 32, 1), pltpu.roll(tile[4], 32, 1)),
        ]
        rest = [(tile[1], 0), (tile[2], 32), (tile[3], 64), (tile[4], 96)]
        last = []
        for core in range(2):
            pieces = [rest[core], rest[core + 2]]
            row16 = None
            for slot in range(4):
                source, at = pieces[slot % 2]
                part = source[16 * (slot // 2) : 16 * (slot // 2) + 16]
                shift = (32 * slot - at) % 128
                part = part if shift == 0 else pltpu.roll(part, shift, 1)
                row16 = part if row16 is None else jnp.where(low < 32 * slot, row16, part)
            last.append(row16)
        for at, zero, one in ((0, main[0], main[1]), (32, main[2], main[3]), (64, last[0], last[1])):
            span = slice(at, at + zero.shape[0])
            keep_ref[place, span] = jnp.where(first, zero, one)
            send_ref[place, span] = jnp.where(first, one, zero).astype(bf16)


def taps_a_kernel(
    core_ref, stats_ref, gain_ref, field_ref, before_ref, cot_ref, after_ref,
    coef_ref, act_ref, padded_ref, send_ref, keep_ref, acc, wide, field, sems,
):
    width, rows = field_ref.shape
    chunks = rows // CHUNK
    pieces = []
    for j in range(chunks):
        lanes = pl.ds(CHUNK * j, CHUNK)
        pieces.append((field_ref.at[:, lanes], field.at[:, lanes]))
    pieces.append((before_ref, padded_ref.at[pl.ds(0, FRAME)]))
    for t in range(rows // FRAME):
        pieces.append(
            (cot_ref.at[pl.ds(FRAME * t, FRAME)], padded_ref.at[pl.ds(FRAME * (t + 1), FRAME)])
        )
    pieces.append((after_ref, padded_ref.at[pl.ds(FRAME + rows, FRAME)]))
    copies = [pltpu.make_async_copy(*piece, sems.at[q]) for q, piece in enumerate(pieces)]
    for copy in copies:
        copy.start()
    total = jnp.sum(stats_ref[...], axis=0)
    mean = total[0:1] * (1.0 / 64)
    gaps = stats_ref[...] - mean[None]
    squares = jnp.sum(gaps * gaps, axis=0)[0:1]
    second = total[1:2] + squares * (CHAN_TOTAL // 64)
    both = jnp.concatenate([mean, second, jnp.zeros((6, 128), f32)], axis=0)
    spread = exact(both, group_columns(128, 0))
    mean, gamma, beta = spread[0:1], gain_ref[0:1, :], gain_ref[1:2, :]
    inv = lax.rsqrt(spread[1:2] * (1.0 / CHAN_TOTAL) + 1e-05)
    coef_ref[...] = jnp.concatenate([mean, inv, gamma, beta, jnp.zeros((4, width), f32)], axis=0)
    coef = jnp.concatenate([mean, inv * gamma, beta, jnp.zeros((5, width), f32)], axis=0).T
    for q in range(3):
        wide[q] = jnp.broadcast_to(coef[:, q : q + 1], (width, 128))

    def activate(j):
        copies[j].wait()
        for at in range(CHUNK * j, CHUNK * j + CHUNK, 128):
            lanes = slice(at, at + 128)
            normed = (field[:, lanes].astype(f32) - wide[0]) * wide[1] + wide[2]
            act_ref[:, lanes] = (normed * sigmoid(normed)).astype(bf16)

    activate(0)
    arrived = chunks
    for j in range(chunks):
        if j + 1 < chunks:
            activate(j + 1)
        needed = chunks + (2 * FRAME + CHUNK * (j + 1) - 1) // FRAME + 1
        for copy in copies[arrived:needed]:
            copy.wait()
        arrived = needed
        add_taps(0, acc, act_ref, padded_ref, j)
    for copy in copies[arrived:]:
        copy.wait()
    acc[960:, :] = jnp.zeros((8, width), f32)
    pack_taps(0, core_ref[0] == 0, acc, send_ref, keep_ref)


def taps_a(core, stats, gain, field_t, before, cot, after):
    width, rows = field_t.shape
    return pl.pallas_call(
        taps_a_kernel,
        in_specs=[IN_SMEM] + [IN_VMEM] * 2 + [ANYWHERE] * 4,
        out_specs=[IN_VMEM] * 5,
        out_shape=[
            jax.ShapeDtypeStruct((8, width), f32),
            vmem((width, rows), bf16),
            vmem((rows + 2 * FRAME, width), bf16),
            jax.ShapeDtypeStruct((32, 80, 128), bf16),
            vmem((32, 80, 128), f32),
        ],
        scratch_shapes=[
            pltpu.VMEM((968, width), f32),
            pltpu.VMEM((3, width, 128), f32),
            pltpu.VMEM((width, rows), bf16),
            pltpu.SemaphoreType.DMA((rows // CHUNK + rows // FRAME + 2,)),
        ],
        compiler_params=params(20),
        cost_estimate=cost(3 * width * rows * width, 10**7, width * rows),
    )(core, stats, gain, *in_hbm(field_t, before, cot, after))


def taps_b_kernel(core_ref, act_ref, padded_ref, send_ref, keep_ref, acc):
    width, rows = act_ref.shape
    for j in range(rows // CHUNK):
        add_taps(1, acc, act_ref, padded_ref, j)
    acc[960:, :] = jnp.zeros((8, width), f32)
    pack_taps(1, core_ref[0] == 0, acc, send_ref, keep_ref)


def taps_b(core, act, padded):
    width, rows = act.shape
    return pl.pallas_call(
        taps_b_kernel,
        in_specs=[IN_SMEM, IN_VMEM, IN_VMEM],
        out_specs=[IN_VMEM] * 2,
        out_shape=[
            jax.ShapeDtypeStruct((32, 80, 128), bf16),
            vmem((32, 80, 128), f32),
        ],
        scratch_shapes=[pltpu.VMEM((968, width), f32)],
        compiler_params=params(16),
        cost_estimate=cost(3 * width * rows * width, 10**7),
    )(core, act, padded)


def merge_kernel(slots, terms, bits_ref, *refs):
    count = len(slots)
    ins, sum_refs, outs = refs[: 2 * count], refs[2 * count : 2 * count + terms], refs[2 * count + terms :]
    for q, slot in enumerate(slots):
        kept_ref, got_ref = ins[2 * q : 2 * q + 2]
        keep_ref, send_ref = outs[2 * q : 2 * q + 2]
        size = keep_ref.shape[0]
        mine, other = pl.ds(bits_ref[slot] * size, size), pl.ds((1 - bits_ref[slot]) * size, size)
        keep_ref[...] = kept_ref[mine] + got_ref[mine].astype(f32)
        send_ref[...] = (kept_ref[other] + got_ref[other].astype(f32)).astype(bf16)
    sums_ref = outs[2 * count]
    if terms == 1:
        sums_ref[...] = sum_refs[0][...]
    else:
        every = lax.broadcasted_iota(jnp.int32, sums_ref.shape, 0) < 15
        here, core, there, both = (ref[...] for ref in sum_refs)
        sums_ref[...] = (here + jnp.where(every, core, 0.0)) + (there + jnp.where(every, both, 0.0))


def merge(bits, chains, sums):
    shapes, args = [], []
    for _, kept, got in chains:
        half_shape = (kept.shape[0] // 2,) + kept.shape[1:]
        shapes += [vmem(half_shape, f32), jax.ShapeDtypeStruct(half_shape, bf16)]
        args += [kept, got]
    shapes.append(jax.ShapeDtypeStruct(sums[0].shape, f32))
    args += sums
    slots = [list(BIT).index(bit) for bit, _, _ in chains]
    out = pl.pallas_call(
        functools.partial(merge_kernel, slots, len(sums)),
        in_specs=[IN_SMEM] + [IN_VMEM] * len(args),
        out_specs=[IN_VMEM] * len(shapes),
        out_shape=shapes,
        compiler_params=params(12),
        cost_estimate=cost(10**5, 10**5),
    )(bits, *args)
    return [(out[2 * q], out[2 * q + 1]) for q in range(len(chains))], out[-1]


def gradient_kernel(
    tie_ref, field_ref, prev_ref, cur_ref, next_ref, kernel_ref, coef_ref, held_ref,
    out_ref, held_out_ref, sums_ref, sums,
):
    step, last = pl.program_id(0), pl.num_programs(0) - 1
    mean, inv, gamma, beta = (coef_ref[q : q + 1, :] for q in range(4))

    @pl.when(step == 0)
    def _():
        sums[...] = held_ref[...]

    rows_by_rows = (((1,), (1,)), ((), ()))
    grad = lax.dot_general(next_ref[...], kernel_ref[0], rows_by_rows, preferred_element_type=f32)
    grad += lax.dot_general(cur_ref[...], kernel_ref[1], rows_by_rows, preferred_element_type=f32)
    grad += lax.dot_general(prev_ref[...], kernel_ref[2], rows_by_rows, preferred_element_type=f32)
    unit = (field_ref[...].astype(f32) - mean) * inv
    normed = unit * gamma + beta
    gate = sigmoid(normed)
    grad = grad * gate * (1.0 + normed * (1.0 - gate))
    out_ref[...] = grad
    sums[0:1, :] += jnp.sum(grad, axis=0, keepdims=True)
    sums[1:2, :] += jnp.sum(grad * unit, axis=0, keepdims=True)
    sums[2:3, :] += jnp.sum(cur_ref[...].astype(f32), axis=0, keepdims=True)

    @pl.when(step == last)
    def _():
        held_out_ref[...] = sums[...]
        for q in range(3):
            for at in range(5):
                sums_ref[5 * q + at : 5 * q + at + 1, :] = sums[q : q + 1, 128 * at : 128 * at + 128]
        weighted = sums[...] * gamma
        sums_ref[15:16, :] = (
            exact(weighted, group_rows(128, 0))[0:1] + exact(weighted, group_rows(128, GROUPS))[1:2]
        )


def gradient(tie, first, field, padded, kernel, coef, held):
    width = field.shape[1]

    def part(at):
        return pl.BlockSpec((FRAME, width), lambda i: (first + i + at, 0))

    top = pl.BlockSpec((8, width), lambda i: (0, 0))
    return pl.pallas_call(
        gradient_kernel,
        grid=(2,),
        in_specs=[
            ANYWHERE,
            part(0),
            part(0),
            part(1),
            part(2),
            pl.BlockSpec(kernel.shape, lambda i: (0, 0, 0)),
            top,
            top,
        ],
        out_specs=[
            pl.BlockSpec((FRAME, width), lambda i: (i, 0)),
            top,
            pl.BlockSpec((16, 128), lambda i: (0, 0)),
        ],
        out_shape=[
            vmem((2 * FRAME, width), f32),
            jax.ShapeDtypeStruct((8, width), f32),
            jax.ShapeDtypeStruct((16, 128), f32),
        ],
        scratch_shapes=[pltpu.VMEM((8, width), f32)],
        compiler_params=params(16),
        cost_estimate=cost(1, 1),
    )(tie, field, padded, padded, padded, kernel, coef, held)


def result_kernel(cot_ref, early_ref, late_ref, field_ref, coef_ref, sums_ref, out_ref, means):
    @pl.when(pl.program_id(0) == 0)
    def _():
        grouped = jnp.broadcast_to(sums_ref[15:16, :], (8, 128)) * (1.0 / CHAN_TOTAL)
        means[0:1, :] = exact(grouped, group_columns(128, 0))[0:1]
        means[1:2, :] = exact(grouped, group_columns(128, GROUPS))[0:1]

    mean, inv, gamma = (coef_ref[q : q + 1, :] for q in range(3))
    unit = (field_ref[...].astype(f32) - mean) * inv
    early = 2 * pl.program_id(0) < pl.num_programs(0)
    for when, grad_ref in ((early, early_ref), (jnp.logical_not(early), late_ref)):

        @pl.when(when)
        def _():
            out_ref[...] = (
                cot_ref[...].astype(f32)
                + inv * (gamma * grad_ref[...] - means[0:1, :] - unit * means[1:2, :])
            ).astype(bf16)


def grad_of_field(cot, early, late, field, coef, sums, block=288):
    rows, width = field.shape
    tile = pl.BlockSpec((block, width), lambda i: (i, 0))
    half_steps = rows // block // 2
    return pl.pallas_call(
        result_kernel,
        grid=(rows // block,),
        in_specs=[
            tile,
            pl.BlockSpec((block, width), lambda i: (jnp.minimum(i, half_steps - 1), 0)),
            pl.BlockSpec((block, width), lambda i: (jnp.maximum(i - half_steps, 0), 0)),
            tile,
            pl.BlockSpec((8, width), lambda i: (0, 0)),
            pl.BlockSpec((16, 128), lambda i: (0, 0)),
        ],
        out_specs=tile,
        out_shape=jax.ShapeDtypeStruct((rows, width), bf16),
        scratch_shapes=[pltpu.VMEM((8, width), f32)],
        compiler_params=params(12),
        cost_estimate=cost(rows * width * 9, rows * width * 10),
    )(cot, early, late, field, coef, sums)


def per_device(field, cotangent, gamma, beta, kernel):
    _, frames, rows, cells, width = field.shape
    loss_scale = 1.0 / math.sqrt(4 * 128 * 18 * 64)
    place = lax.axis_index(AXES)
    own = {name: (place >> bit) & 1 for name, bit in BIT.items()}
    off = {name: 1 - bit for name, bit in own.items()}
    bits = jnp.stack(list(own.values()) + list(off.values())).astype(jnp.int32)
    core = own["core"].astype(jnp.int32).reshape(1)
    gain = jnp.concatenate([gamma[None], beta[None], jnp.zeros((6, width), f32)], axis=0)

    flat, cot = field.reshape(-1, width), cotangent.reshape(-1, width)
    stats, first, final = local_stats(bits, flat, cot)
    up = [(i, i + 1) for i in range(31)]
    before = lax.ppermute(final, "tm", up)
    after = lax.ppermute(first, "tm", [(j, i) for i, j in up])
    stats = lax.all_to_all(stats, ("tm", "height"), 0, 0)
    field_t = turned(flat)

    coef, act_t, padded, send_a, keep_a = taps_a(core, stats, gain, field_t, before, cot, after)
    got_a = swap(send_a, "core")
    send_b, keep_b = taps_b(core, act_t, padded)
    got_b = swap(send_b, "core")
    none = jnp.zeros((8, width), f32)
    grad_early, held, _ = gradient(keep_b, 0, flat, padded, kernel, coef, none)
    kept, got = [keep_a, keep_b], [got_a, got_b]
    sums = [held]
    for step in range(3):
        merged, sums = merge(bits, [(ORDERS[q][step], kept[q], got[q]) for q in range(2)], sums)
        kept = [merged[q][0] for q in range(2)]
        got = [
            lax.ppermute(merged[q][1], AXES, neighbours(NEAR[ORDERS[q][step]])) for q in range(2)
        ]
        if step == 0:
            grad_late, _, sums = gradient(kept[0], 2, flat, padded, kernel, coef, sums)
            sums = [sums]
        elif step == 1:
            sums = [sums, swap(sums, "core"), swap(sums, "z0"), swap(sums, "core", "z0")]
        else:
            sums = (sums + swap(sums, "x0")) + (swap(sums, "yl") + swap(sums, "x0", "yl"))
    taps = jnp.stack([kept[q] + got[q].astype(f32) for q in range(2)])
    taps = taps.reshape(2, 2, 2, 80, 128)
    taps, sums = far_halve(taps, 2, "z1", own, off, sums)
    taps, sums = far_halve(taps, 1, "x1", own, off, sums)
    taps, sums = far_halve(taps, 0, "z2", own, off, sums)
    field_grad = grad_of_field(cot, grad_early, grad_late, flat, coef, sums)

    got, sums = far_swap(taps, sums, "yh")
    taps = taps + got
    main = half(taps[:64].reshape(2, 32, 128), 0, own["yh"])
    rest = half(taps[64:].reshape(16, 2, 2, 32), 2, own["yh"])
    rest = jnp.concatenate([rest[:, 0], rest[:, 1]], axis=0)
    kernel_grad = jnp.concatenate([main, rest], axis=1)[:30] * loss_scale
    channel_grads = sums[:15].reshape(3, width) * loss_scale
    return (field_grad.reshape(field.shape), kernel_grad, channel_grads)


def solution(mesh):
    spread = P("dp", "tm", "height", None, None)
    return jax.shard_map(
        per_device,
        mesh=mesh,
        in_specs=(spread, spread, P(), P(), P()),
        out_specs=(spread, P(("tm", "height"), "dp"), P()),
        check_vma=False,
    )
```

```python
import functools
import math

import jax
import jax.numpy as jnp
from jax import lax
from jax.experimental import pallas as pl
from jax.experimental.pallas import tpu as pltpu
from jax.sharding import PartitionSpec as P

GROUPS = 32
CPG = 20
FRAME = 576
CHUNK = 768
CHAN_TOTAL = 128 * 18 * 64 * CPG
AXES = ("dp", "tm", "height")
BIT = {"yh": 7, "core": 6, "x1": 5, "x0": 4, "z2": 3, "z1": 2, "z0": 1, "yl": 0}
OWNER = ("x1", "x0", "z2", "z1", "z0", "yl")
ORDERS = (("z0", "x0", "yl", "x1", "z1"), ("yl", "z0", "x0", "x1", "z1"))
f32 = jnp.float32
bf16 = jnp.bfloat16
IN_VMEM = pl.BlockSpec(memory_space=pltpu.VMEM)
ANYWHERE = pl.BlockSpec(memory_space=pl.ANY)
IN_SMEM = pl.BlockSpec(memory_space=pltpu.SMEM)


def params(mib):
    return pltpu.CompilerParams(vmem_limit_bytes=mib * 2**20)


def vmem(shape, dtype):
    return pltpu.VMEM(shape, dtype)


def in_hbm(*arrays):
    return [pltpu.with_memory_space_constraint(array, pltpu.HBM) for array in arrays]


def cost(flops, moved, transcendentals=0):
    return pl.CostEstimate(flops=flops, bytes_accessed=moved, transcendentals=transcendentals)


def pairs(bits):
    mask = sum(1 << BIT[bit] for bit in bits)
    return [(i, i ^ mask) for i in range(256)]


def neighbours(axis):
    out = []
    for i in range(256):
        bit = {name: (i >> at) & 1 for name, at in BIT.items()}
        x, y = 2 * bit["x1"] + bit["x0"], 2 * bit["yh"] + bit["yl"]
        z = 4 * bit["z2"] + 2 * bit["z1"] + bit["z0"]
        place = {"x": x, "y": y, "z": z}
        size = 8 if axis == "z" else 4
        at = place[axis]
        step = 1 if (at % 2 == 0) == (bit["core"] == 0) else -1
        place[axis] = (at + step) % size
        x, y, z = place["x"], place["y"], place["z"]
        out.append((i, (((y >> 1) * 2 + bit["core"]) * 32 + x * 8 + z) * 2 + (y & 1)))
    return out


NEAR = {"z0": "z", "x0": "x", "yl": "y"}


def swap(value, *bits):
    chosen = pairs(bits)
    if bits == ("z1",):
        both = pairs(("z1", "z2"))
        chosen = [both[i] if (i >> BIT["core"]) & 1 else pair for i, pair in enumerate(chosen)]
    return lax.ppermute(value, AXES, chosen)


def half(total, axis, index):
    return lax.dynamic_index_in_dim(total, index, axis, False, allow_negative_indices=False)


def far_swap(send, sums, bit):
    high = lax.reduce_precision(sums, 8, 7)
    rest = sums - high
    middle = lax.reduce_precision(rest, 8, 7)
    parts = [part.astype(bf16) for part in (high, middle, rest - middle)]
    rows = send.reshape(-1, 128)
    got = swap(jnp.concatenate([rows.astype(bf16)] + parts, axis=0), bit).astype(f32)
    cut, count = rows.shape[0], sums.shape[0]
    other = [got[cut + i * count : cut + (i + 1) * count] for i in range(3)]
    return got[:cut].reshape(send.shape), sums + (other[0] + (other[1] + other[2]))


def far_halve(total, axis, bit, own, off, sums):
    keep = half(total, axis, own[bit])
    send = half(total, axis, off[bit])
    got, sums = far_swap(send, sums, bit)
    return keep + got, sums


def group_rows(lanes, first):
    channel = lax.broadcasted_iota(jnp.int32, (640, lanes), 0)
    start = (lax.broadcasted_iota(jnp.int32, (640, lanes), 1) - first) * CPG
    return jnp.where((channel >= start) & (channel < start + CPG), 1.0, 0.0).astype(f32)


def group_columns(rows, first):
    channel = lax.broadcasted_iota(jnp.int32, (rows, 640), 1)
    start = (lax.broadcasted_iota(jnp.int32, (rows, 640), 0) - first) * CPG
    return jnp.where((channel >= start) & (channel < start + CPG), 1.0, 0.0).astype(f32)


def exact(left, right):
    return jnp.dot(left, right, preferred_element_type=f32, precision=lax.Precision.HIGHEST)


def stats_kernel(
    bits_ref, upper_ref, lower_ref, head_ref, tail_ref, out_ref, first_ref, final_ref, means, seconds
):
    step, last = pl.program_id(0), pl.num_programs(0) - 1
    count = upper_ref.shape[0]
    @pl.when(step == 0)
    def _():
        first_ref[...] = head_ref[...]
        final_ref[...] = tail_ref[...]
        means[...] = jnp.zeros_like(means)
        seconds[...] = jnp.zeros_like(seconds)

    for part, ref in enumerate((upper_ref, lower_ref)):
        mean = jnp.sum(ref[...].astype(f32), axis=0, keepdims=True) * (1.0 / count)
        gap = ref[...].astype(f32) - mean
        means[pl.ds(2 * step + part, 1), :] = mean
        seconds[0:1, :] += jnp.sum(gap * gap, axis=0, keepdims=True)

    @pl.when(step == last)
    def _():
        blocks = BLOCKS
        total = jnp.sum(means[...], axis=0, keepdims=True) * (1.0 / blocks)
        to_groups, to_channels = group_rows(128, 0), group_columns(128, 0)
        eight = jnp.broadcast_to(total, (8, total.shape[1]))
        mean = exact(eight, to_groups) * (1.0 / CPG)
        gaps = means[0:blocks, :] - exact(mean, to_channels)[0:1]
        spread = seconds[0:1, :] + count * jnp.sum(gaps * gaps, axis=0, keepdims=True)
        second = exact(jnp.broadcast_to(spread, eight.shape), to_groups)
        both = jnp.concatenate([mean[0:1], second[0:1]], axis=0)
        out_ref[...] = jnp.broadcast_to(both[None], out_ref.shape)


BLOCKS = 6


def local_stats(bits, field, cot):
    rows, width = field.shape
    block = rows // BLOCKS
    field = pltpu.with_memory_space_constraint(field, pltpu.HBM)
    return pl.pallas_call(
        stats_kernel,
        grid=(BLOCKS // 2,),
        in_specs=[
            IN_SMEM,
            pl.BlockSpec((block, width), lambda i: (2 * i, 0)),
            pl.BlockSpec((block, width), lambda i: (2 * i + 1, 0)),
            pl.BlockSpec((FRAME, width), lambda i: (0, 0)),
            pl.BlockSpec((FRAME, width), lambda i: (rows // FRAME - 1, 0)),
        ],
        out_specs=[
            pl.BlockSpec((64, 2, 128), lambda i: (0, 0, 0)),
            pl.BlockSpec((FRAME, width), lambda i: (0, 0)),
            pl.BlockSpec((FRAME, width), lambda i: (0, 0)),
        ],
        out_shape=[
            jax.ShapeDtypeStruct((64, 2, 128), f32),
            pltpu.HBM((FRAME, width), bf16),
            pltpu.HBM((FRAME, width), bf16),
        ],
        scratch_shapes=[
            pltpu.VMEM((8, width), f32),
            pltpu.VMEM((8, width), f32),
        ],
        compiler_params=params(16),
        cost_estimate=cost(rows * width * 4, rows * width * 2),
    )(bits, field, field, *in_hbm(cot, cot))


def turn_kernel(field_ref, turned_ref):
    turned_ref[...] = field_ref[...].T


def turned(field):
    rows, width = field.shape
    return pl.pallas_call(
        turn_kernel,
        grid=(width // 128,),
        in_specs=[pl.BlockSpec((rows, 128), lambda i: (0, i))],
        out_specs=pl.BlockSpec((128, rows), lambda i: (i, 0)),
        out_shape=pltpu.HBM((width, rows), bf16),
        compiler_params=params(12),
        cost_estimate=cost(10**9, 10**7),
    )(field)


def grad_act_kernel(prev_ref, cur_ref, next_ref, kernel_ref, out_ref):
    out_ref[...] = frame_grad_act(prev_ref[...], cur_ref[...], next_ref[...], kernel_ref)


def frame_grad_act(before, here, after, kernel_ref):
    rows_by_rows = (((1,), (1,)), ((), ()))
    out = lax.dot_general(after, kernel_ref[0], rows_by_rows, preferred_element_type=f32)
    out += lax.dot_general(here, kernel_ref[1], rows_by_rows, preferred_element_type=f32)
    return out + lax.dot_general(before, kernel_ref[2], rows_by_rows, preferred_element_type=f32)


def inner_grad_act(cot, kernel):
    width = cot.shape[1]

    def part(at):
        return pl.BlockSpec((FRAME, width), lambda i: (i + at, 0))

    return pl.pallas_call(
        grad_act_kernel,
        grid=(2,),
        in_specs=[part(0), part(1), part(2), pl.BlockSpec(kernel.shape, lambda i: (0, 0, 0))],
        out_specs=pl.BlockSpec((FRAME, width), lambda i: (i, 0)),
        out_shape=pltpu.HBM((2 * FRAME, width), f32),
        compiler_params=params(20),
        cost_estimate=cost(10**9, 10**7),
    )(*in_hbm(cot, cot, cot, kernel))


def owners(chain):
    out = []
    for block in range(64):
        bit = {name: (block >> (5 - i)) & 1 for i, name in enumerate(OWNER)}
        if bit["z2"] == chain:
            place = 0
            for name in ORDERS[chain]:
                place = 2 * place + bit[name]
            out.append((block, place))
    return out


def segments(chain):
    parts = {}
    for start in range(240 * chain, 1920, 480):
        row = start
        while row < start + 240:
            tap, channel = divmod(row, 640)
            length = min(start + 240 - row, 640 - channel)
            parts.setdefault(tap, []).append((channel, length))
            row += length
    out, at = [], 0
    for tap in sorted(parts):
        out.append((tap, tuple(parts[tap]), at))
        at += sum(length for _, length in parts[tap])
    return out


def add_taps(chain, acc, act_ref, cot_ref, j):
    lanes = slice(CHUNK * j, CHUNK * j + CHUNK)
    for tap, parts, at in segments(chain):
        start = FRAME * (2 - tap) + CHUNK * j
        rows = [act_ref[channel : channel + length, lanes] for channel, length in parts]
        rows = rows[0] if len(rows) == 1 else jnp.concatenate(rows, axis=0)
        part = jnp.dot(rows, cot_ref[start : start + CHUNK, :], preferred_element_type=f32)
        if j == 0:
            acc[at : at + rows.shape[0], :] = part
        else:
            acc[at : at + rows.shape[0], :] += part


def pack_taps(chain, first, acc, send_ref, keep_ref):
    lane = lax.broadcasted_iota(jnp.int32, (32, 128), 1)
    low = lax.broadcasted_iota(jnp.int32, (16, 128), 1)
    for number, (_, place) in enumerate(owners(chain)):
        rows = slice(30 * number, 30 * number + 32)
        tile = [acc[rows, 128 * q : 128 * q + 128] for q in range(5)]
        main = [
            tile[0],
            jnp.where(lane < 96, pltpu.roll(tile[1], 96, 1), pltpu.roll(tile[2], 96, 1)),
            jnp.where(lane < 64, pltpu.roll(tile[2], 64, 1), pltpu.roll(tile[3], 64, 1)),
            jnp.where(lane < 32, pltpu.roll(tile[3], 32, 1), pltpu.roll(tile[4], 32, 1)),
        ]
        rest = [(tile[1], 0), (tile[2], 32), (tile[3], 64), (tile[4], 96)]
        last = []
        for core in range(2):
            pieces = [rest[core], rest[core + 2]]
            row16 = None
            for slot in range(4):
                source, at = pieces[slot % 2]
                part = source[16 * (slot // 2) : 16 * (slot // 2) + 16]
                shift = (32 * slot - at) % 128
                part = part if shift == 0 else pltpu.roll(part, shift, 1)
                row16 = part if row16 is None else jnp.where(low < 32 * slot, row16, part)
            last.append(row16)
        for at, zero, one in ((0, main[0], main[1]), (32, main[2], main[3]), (64, last[0], last[1])):
            span = slice(at, at + zero.shape[0])
            keep_ref[place, span] = jnp.where(first, zero, one)
            send_ref[place, span] = jnp.where(first, one, zero).astype(bf16)


def taps_a_kernel(
    core_ref, stats_ref, gain_ref, field_ref, before_ref, cot_ref, after_ref, tie_ref,
    coef_ref, act_ref, padded_ref, send_ref, keep_ref, acc, wide, field, sems,
):
    width, rows = field_ref.shape
    chunks = rows // CHUNK
    pieces = []
    for j in range(chunks):
        lanes = pl.ds(CHUNK * j, CHUNK)
        pieces.append((field_ref.at[:, lanes], field.at[:, lanes]))
    pieces.append((before_ref, padded_ref.at[pl.ds(0, FRAME)]))
    for t in range(rows // FRAME):
        pieces.append(
            (cot_ref.at[pl.ds(FRAME * t, FRAME)], padded_ref.at[pl.ds(FRAME * (t + 1), FRAME)])
        )
    pieces.append((after_ref, padded_ref.at[pl.ds(FRAME + rows, FRAME)]))
    copies = [pltpu.make_async_copy(*piece, sems.at[q]) for q, piece in enumerate(pieces)]
    copies[0].start()
    total = jnp.sum(stats_ref[...], axis=0)
    mean = total[0:1] * (1.0 / 64)
    gaps = stats_ref[...] - mean[None]
    squares = jnp.sum(gaps * gaps, axis=0)[0:1]
    second = total[1:2] + squares * (CHAN_TOTAL // 64)
    both = jnp.concatenate([mean, second, jnp.zeros((6, 128), f32)], axis=0)
    spread = exact(both, group_columns(128, 0))
    mean, gamma, beta = spread[0:1], gain_ref[0:1, :], gain_ref[1:2, :]
    inv = lax.rsqrt(spread[1:2] * (1.0 / CHAN_TOTAL) + 1e-05)
    coef_ref[...] = jnp.concatenate([mean, inv, gamma, beta, jnp.zeros((4, width), f32)], axis=0)
    scaled = [mean, 0.5 * inv * gamma, 0.5 * beta, jnp.zeros((5, width), f32)]
    coef = jnp.concatenate(scaled, axis=0).T
    for q in range(3):
        wide[q] = jnp.broadcast_to(coef[:, q : q + 1], (width, 128))

    copies[0].wait()
    for q in [1] + list(range(chunks, len(copies) - 2)) + list(range(2, chunks)):
        copies[q].start()
    for copy in copies[-2:]:
        copy.start()

    def activate(j):
        if j > 0:
            copies[j].wait()
        for at in range(CHUNK * j, CHUNK * j + CHUNK, 128):
            lanes = slice(at, at + 128)
            half_normed = (field[:, lanes].astype(f32) - wide[0]) * wide[1] + wide[2]
            act_ref[:, lanes] = (half_normed + half_normed * jnp.tanh(half_normed)).astype(bf16)

    activate(0)
    arrived = chunks
    for j in range(chunks):
        if j + 1 < chunks:
            activate(j + 1)
        needed = chunks + (2 * FRAME + CHUNK * (j + 1) - 1) // FRAME + 1
        for copy in copies[arrived:needed]:
            copy.wait()
        arrived = needed
        add_taps(0, acc, act_ref, padded_ref, j)
    for copy in copies[arrived:]:
        copy.wait()
    acc[960:, :] = jnp.zeros((8, width), f32)
    pack_taps(0, core_ref[0] == 0, acc, send_ref, keep_ref)


def taps_a(core, stats, gain, field_t, before, cot, after, tie):
    width, rows = field_t.shape
    return pl.pallas_call(
        taps_a_kernel,
        in_specs=[IN_SMEM] + [IN_VMEM] * 2 + [ANYWHERE] * 5,
        out_specs=[IN_VMEM] * 5,
        out_shape=[
            jax.ShapeDtypeStruct((8, width), f32),
            vmem((width, rows), bf16),
            vmem((rows + 2 * FRAME, width), bf16),
            jax.ShapeDtypeStruct((32, 80, 128), bf16),
            vmem((32, 80, 128), f32),
        ],
        scratch_shapes=[
            pltpu.VMEM((968, width), f32),
            pltpu.VMEM((3, width, 128), f32),
            pltpu.VMEM((width, rows), bf16),
            pltpu.SemaphoreType.DMA((rows // CHUNK + rows // FRAME + 2,)),
        ],
        compiler_params=params(20),
        cost_estimate=cost(3 * width * rows * width, 10**7, width * rows),
    )(core, stats, gain, *in_hbm(field_t, before, cot, after, tie))


def taps_b_kernel(core_ref, act_ref, padded_ref, send_ref, keep_ref, acc):
    width, rows = act_ref.shape
    for j in range(rows // CHUNK):
        add_taps(1, acc, act_ref, padded_ref, j)
    acc[960:, :] = jnp.zeros((8, width), f32)
    pack_taps(1, core_ref[0] == 0, acc, send_ref, keep_ref)


def taps_b(core, act, padded):
    width, rows = act.shape
    return pl.pallas_call(
        taps_b_kernel,
        in_specs=[IN_SMEM, IN_VMEM, IN_VMEM],
        out_specs=[IN_VMEM] * 2,
        out_shape=[
            jax.ShapeDtypeStruct((32, 80, 128), bf16),
            vmem((32, 80, 128), f32),
        ],
        scratch_shapes=[pltpu.VMEM((968, width), f32)],
        compiler_params=params(16),
        cost_estimate=cost(3 * width * rows * width, 10**7),
    )(core, act, padded)


def merge_kernel(slots, terms, bits_ref, *refs):
    count = len(slots)
    ins, sum_refs, outs = refs[: 2 * count], refs[2 * count : 2 * count + terms], refs[2 * count + terms :]
    for q, slot in enumerate(slots):
        kept_ref, got_ref = ins[2 * q : 2 * q + 2]
        keep_ref, send_ref = outs[2 * q : 2 * q + 2]
        size = keep_ref.shape[0]
        mine, other = pl.ds(bits_ref[slot] * size, size), pl.ds((1 - bits_ref[slot]) * size, size)
        keep_ref[...] = kept_ref[mine] + got_ref[mine].astype(f32)
        send_ref[...] = (kept_ref[other] + got_ref[other].astype(f32)).astype(bf16)
    sums_ref = outs[2 * count]
    if terms == 1:
        sums_ref[...] = sum_refs[0][...]
    else:
        every = lax.broadcasted_iota(jnp.int32, sums_ref.shape, 0) < 15
        here, core, there, both = (ref[...] for ref in sum_refs)
        sums_ref[...] = (here + jnp.where(every, core, 0.0)) + (there + jnp.where(every, both, 0.0))


def merge(bits, chains, sums):
    shapes, args = [], []
    for _, kept, got in chains:
        half_shape = (kept.shape[0] // 2,) + kept.shape[1:]
        shapes += [vmem(half_shape, f32), jax.ShapeDtypeStruct(half_shape, bf16)]
        args += [kept, got]
    shapes.append(jax.ShapeDtypeStruct(sums[0].shape, f32))
    args += sums
    slots = [list(BIT).index(bit) for bit, _, _ in chains]
    out = pl.pallas_call(
        functools.partial(merge_kernel, slots, len(sums)),
        in_specs=[IN_SMEM] + [IN_VMEM] * len(args),
        out_specs=[IN_VMEM] * len(shapes),
        out_shape=shapes,
        compiler_params=params(12),
        cost_estimate=cost(10**5, 10**5),
    )(bits, *args)
    return [(out[2 * q], out[2 * q + 1]) for q in range(len(chains))], out[-1]


def gradient_kernel(
    inner, tie_ref, field_ref, padded_ref, kernel_ref, coef_ref, held_ref,
    out_ref, held_out_ref, sums_ref, sums,
):
    step, last = pl.program_id(0), pl.num_programs(0) - 1
    mean, inv, gamma, beta = (coef_ref[q : q + 1, :] for q in range(4))

    @pl.when(step == 0)
    def _():
        sums[...] = held_ref[...]

    frame = 1 + step if inner else 3 * step
    near = [
        padded_ref[pl.ds(pl.multiple_of((frame + t) * FRAME, FRAME), FRAME), :]
        for t in ((1,) if inner else (0, 1, 2))
    ]
    cot = near[len(near) // 2].astype(f32)
    grad = kernel_ref[...] if inner else frame_grad_act(*near, kernel_ref)
    unit = (field_ref[...].astype(f32) - mean) * inv
    half_normed = unit * (0.5 * gamma) + 0.5 * beta
    turn = jnp.tanh(half_normed)
    grad = grad * (0.5 * ((1.0 + turn) + half_normed * (1.0 - turn * turn)))
    out_ref[pl.ds(pl.multiple_of(step * FRAME, FRAME), FRAME), :] = cot + (inv * gamma) * grad
    sums[0:1, :] += jnp.sum(grad, axis=0, keepdims=True)
    sums[1:2, :] += jnp.sum(grad * unit, axis=0, keepdims=True)
    sums[2:3, :] += jnp.sum(cot, axis=0, keepdims=True)

    @pl.when(step == last)
    def _():
        held_out_ref[...] = sums[...]
        for q in range(3):
            for at in range(5):
                sums_ref[5 * q + at : 5 * q + at + 1, :] = sums[q : q + 1, 128 * at : 128 * at + 128]
        weighted = sums[...] * gamma
        sums_ref[15:16, :] = (
            exact(weighted, group_rows(128, 0))[0:1] + exact(weighted, group_rows(128, GROUPS))[1:2]
        )


def gradient(tie, inner, field, padded, kernel, coef, held):
    width = field.shape[1]

    top = pl.BlockSpec((8, width), lambda i: (0, 0))
    return pl.pallas_call(
        functools.partial(gradient_kernel, inner),
        grid=(2,),
        in_specs=[
            ANYWHERE,
            pl.BlockSpec((FRAME, width), lambda i: (1 + i if inner else 3 * i, 0)),
            IN_VMEM,
            pl.BlockSpec((FRAME, width), lambda i: (i, 0)) if inner else IN_VMEM,
            top,
            top,
        ],
        out_specs=[
            IN_VMEM,
            top,
            pl.BlockSpec((16, 128), lambda i: (0, 0)),
        ],
        out_shape=[
            vmem((2 * FRAME, width), f32),
            jax.ShapeDtypeStruct((8, width), f32),
            jax.ShapeDtypeStruct((16, 128), f32),
        ],
        scratch_shapes=[pltpu.VMEM((8, width), f32)],
        compiler_params=params(16),
        cost_estimate=cost(1, 1),
    )(tie, field, padded, kernel, coef, held)


def result_kernel(inner_ref, outer_ref, field_ref, coef_ref, sums_ref, out_ref, means):
    @pl.when(pl.program_id(0) == 0)
    def _():
        grouped = jnp.broadcast_to(sums_ref[15:16, :], (8, 128)) * (1.0 / CHAN_TOTAL)
        means[0:1, :] = exact(grouped, group_columns(128, 0))[0:1]
        means[1:2, :] = exact(grouped, group_columns(128, GROUPS))[0:1]

    size, step = out_ref.shape[0], pl.program_id(0)
    per_frame = FRAME // size
    inner = (step >= per_frame) & (step < 3 * per_frame)
    before = jnp.where(inner, per_frame, jnp.where(step < per_frame, 0, 2 * per_frame))
    rows = pl.ds(pl.multiple_of((step - before) * size, size), size)
    mean, inv = coef_ref[0:1, :], coef_ref[1:2, :]
    unit = (field_ref[...].astype(f32) - mean) * inv
    taken = inv * (means[0:1, :] + unit * means[1:2, :])
    for when, grad_ref in ((inner, inner_ref), (jnp.logical_not(inner), outer_ref)):

        @pl.when(when)
        def _():
            out_ref[...] = (grad_ref[rows, :] - taken).astype(bf16)


def grad_of_field(inner, outer, field, coef, sums, block=288):
    rows, width = field.shape
    tile = pl.BlockSpec((block, width), lambda i: (i, 0))
    return pl.pallas_call(
        result_kernel,
        grid=(rows // block,),
        in_specs=[
            IN_VMEM,
            IN_VMEM,
            tile,
            pl.BlockSpec((8, width), lambda i: (0, 0)),
            pl.BlockSpec((16, 128), lambda i: (0, 0)),
        ],
        out_specs=tile,
        out_shape=jax.ShapeDtypeStruct((rows, width), bf16),
        scratch_shapes=[pltpu.VMEM((8, width), f32)],
        compiler_params=params(12),
        cost_estimate=cost(rows * width * 9, rows * width * 10),
    )(inner, outer, field, coef, sums)


def per_device(field, cotangent, gamma, beta, kernel):
    _, frames, rows, cells, width = field.shape
    loss_scale = 1.0 / math.sqrt(4 * 128 * 18 * 64)
    place = lax.axis_index(AXES)
    own = {name: (place >> bit) & 1 for name, bit in BIT.items()}
    off = {name: 1 - bit for name, bit in own.items()}
    bits = jnp.stack(list(own.values()) + list(off.values())).astype(jnp.int32)
    core = own["core"].astype(jnp.int32).reshape(1)
    gain = jnp.concatenate([gamma[None], beta[None], jnp.zeros((6, width), f32)], axis=0)

    flat, cot = field.reshape(-1, width), cotangent.reshape(-1, width)
    stats, first, final = local_stats(bits, flat, cot)
    up = [(i, i + 1) for i in range(31)]
    before = lax.ppermute(final, "tm", up)
    after = lax.ppermute(first, "tm", [(j, i) for i, j in up])
    stats = lax.all_to_all(stats, ("tm", "height"), 0, 0)
    field_t = turned(flat)
    grad_inner = inner_grad_act(cot, kernel)

    coef, act_t, padded, send_a, keep_a = taps_a(
        core, stats, gain, field_t, before, cot, after, grad_inner
    )
    got_a = swap(send_a, "core")
    send_b, keep_b = taps_b(core, act_t, padded)
    got_b = swap(send_b, "core")
    none = jnp.zeros((8, width), f32)
    inner, held, _ = gradient(keep_b, True, flat, padded, grad_inner, coef, none)
    kept, got = [keep_a, keep_b], [got_a, got_b]
    sums = [held]
    for step in range(3):
        merged, sums = merge(bits, [(ORDERS[q][step], kept[q], got[q]) for q in range(2)], sums)
        kept = [merged[q][0] for q in range(2)]
        got = [
            lax.ppermute(merged[q][1], AXES, neighbours(NEAR[ORDERS[q][step]])) for q in range(2)
        ]
        if step == 0:
            outer, _, sums = gradient(kept[0], False, flat, padded, kernel, coef, sums)
            sums = [sums]
        elif step == 1:
            sums = [sums, swap(sums, "core"), swap(sums, "z0"), swap(sums, "core", "z0")]
        else:
            sums = (sums + swap(sums, "x0")) + (swap(sums, "yl") + swap(sums, "x0", "yl"))
    taps = jnp.stack([kept[q] + got[q].astype(f32) for q in range(2)])
    taps = taps.reshape(2, 2, 2, 80, 128)
    taps, sums = far_halve(taps, 2, "z1", own, off, sums)
    taps, sums = far_halve(taps, 1, "x1", own, off, sums)
    taps, sums = far_halve(taps, 0, "z2", own, off, sums)
    field_grad = grad_of_field(inner, outer, flat, coef, sums)

    got, sums = far_swap(taps, sums, "yh")
    taps = taps + got
    main = half(taps[:64].reshape(2, 32, 128), 0, own["yh"])
    rest = half(taps[64:].reshape(16, 2, 2, 32), 2, own["yh"])
    rest = jnp.concatenate([rest[:, 0], rest[:, 1]], axis=0)
    kernel_grad = jnp.concatenate([main, rest], axis=1)[:30] * loss_scale
    channel_grads = sums[:15].reshape(3, width) * loss_scale
    return (field_grad.reshape(field.shape), kernel_grad, channel_grads)


def solution(mesh):
    spread = P("dp", "tm", "height", None, None)
    return jax.shard_map(
        per_device,
        mesh=mesh,
        in_specs=(spread, spread, P(), P(), P()),
        out_specs=(spread, P(("tm", "height"), "dp"), P()),
        check_vma=False,
    )
```

```python
import functools
import math

import jax
import jax.numpy as jnp
from jax import lax
from jax.experimental import pallas as pl
from jax.experimental.pallas import tpu as pltpu
from jax.sharding import PartitionSpec as P

GROUPS = 32
CPG = 20
FRAME = 576
CHUNK = 768
CHAN_TOTAL = 128 * 18 * 64 * CPG
AXES = ("dp", "tm", "height")
BIT = {"yh": 7, "core": 6, "x1": 5, "x0": 4, "z2": 3, "z1": 2, "z0": 1, "yl": 0}
OWNER = ("x1", "x0", "z2", "z1", "z0", "yl")
ORDERS = (("z0", "x0", "yl", "x1", "z1"), ("yl", "z0", "x0", "x1", "z1"))
f32 = jnp.float32
bf16 = jnp.bfloat16
IN_VMEM = pl.BlockSpec(memory_space=pltpu.VMEM)
ANYWHERE = pl.BlockSpec(memory_space=pl.ANY)
IN_SMEM = pl.BlockSpec(memory_space=pltpu.SMEM)


def params(mib):
    return pltpu.CompilerParams(vmem_limit_bytes=mib * 2**20)


def vmem(shape, dtype):
    return pltpu.VMEM(shape, dtype)


def in_hbm(*arrays):
    return [pltpu.with_memory_space_constraint(array, pltpu.HBM) for array in arrays]


def cost(flops, moved, transcendentals=0):
    return pl.CostEstimate(flops=flops, bytes_accessed=moved, transcendentals=transcendentals)


def pairs(bits):
    mask = sum(1 << BIT[bit] for bit in bits)
    return [(i, i ^ mask) for i in range(256)]


def neighbours(axis):
    out = []
    for i in range(256):
        bit = {name: (i >> at) & 1 for name, at in BIT.items()}
        x, y = 2 * bit["x1"] + bit["x0"], 2 * bit["yh"] + bit["yl"]
        z = 4 * bit["z2"] + 2 * bit["z1"] + bit["z0"]
        place = {"x": x, "y": y, "z": z}
        size = 8 if axis == "z" else 4
        at = place[axis]
        step = 1 if (at % 2 == 0) == (bit["core"] == 0) else -1
        place[axis] = (at + step) % size
        x, y, z = place["x"], place["y"], place["z"]
        out.append((i, (((y >> 1) * 2 + bit["core"]) * 32 + x * 8 + z) * 2 + (y & 1)))
    return out


NEAR = {"z0": "z", "x0": "x", "yl": "y"}


def swap(value, *bits):
    chosen = pairs(bits)
    if bits == ("z1",):
        both = pairs(("z1", "z2"))
        chosen = [both[i] if (i >> BIT["core"]) & 1 else pair for i, pair in enumerate(chosen)]
    return lax.ppermute(value, AXES, chosen)


def half(total, axis, index):
    return lax.dynamic_index_in_dim(total, index, axis, False, allow_negative_indices=False)


def far_swap(send, sums, bit):
    high = lax.reduce_precision(sums, 8, 7)
    rest = sums - high
    middle = lax.reduce_precision(rest, 8, 7)
    parts = [part.astype(bf16) for part in (high, middle, rest - middle)]
    rows = send.reshape(-1, 128)
    got = swap(jnp.concatenate([rows.astype(bf16)] + parts, axis=0), bit).astype(f32)
    cut, count = rows.shape[0], sums.shape[0]
    other = [got[cut + i * count : cut + (i + 1) * count] for i in range(3)]
    return got[:cut].reshape(send.shape), sums + (other[0] + (other[1] + other[2]))


def far_halve(total, axis, bit, own, off, sums):
    keep = half(total, axis, own[bit])
    send = half(total, axis, off[bit])
    got, sums = far_swap(send, sums, bit)
    return keep + got, sums


def group_rows(lanes, first):
    channel = lax.broadcasted_iota(jnp.int32, (640, lanes), 0)
    start = (lax.broadcasted_iota(jnp.int32, (640, lanes), 1) - first) * CPG
    return jnp.where((channel >= start) & (channel < start + CPG), 1.0, 0.0).astype(f32)


def group_columns(rows, first):
    channel = lax.broadcasted_iota(jnp.int32, (rows, 640), 1)
    start = (lax.broadcasted_iota(jnp.int32, (rows, 640), 0) - first) * CPG
    return jnp.where((channel >= start) & (channel < start + CPG), 1.0, 0.0).astype(f32)


def exact(left, right):
    return jnp.dot(left, right, preferred_element_type=f32, precision=lax.Precision.HIGHEST)


def stats_kernel(
    bits_ref, upper_ref, lower_ref, head_ref, tail_ref, out_ref, first_ref, final_ref, means, seconds
):
    step, last = pl.program_id(0), pl.num_programs(0) - 1
    count = upper_ref.shape[0]
    @pl.when(step == 0)
    def _():
        first_ref[...] = head_ref[...]
        final_ref[...] = tail_ref[...]
        means[...] = jnp.zeros_like(means)
        seconds[...] = jnp.zeros_like(seconds)

    for part, ref in enumerate((upper_ref, lower_ref)):
        mean = jnp.sum(ref[...].astype(f32), axis=0, keepdims=True) * (1.0 / count)
        gap = ref[...].astype(f32) - mean
        means[pl.ds(2 * step + part, 1), :] = mean
        seconds[0:1, :] += jnp.sum(gap * gap, axis=0, keepdims=True)

    @pl.when(step == last)
    def _():
        blocks = BLOCKS
        total = jnp.sum(means[...], axis=0, keepdims=True) * (1.0 / blocks)
        to_groups, to_channels = group_rows(128, 0), group_columns(128, 0)
        eight = jnp.broadcast_to(total, (8, total.shape[1]))
        mean = exact(eight, to_groups) * (1.0 / CPG)
        gaps = means[0:blocks, :] - exact(mean, to_channels)[0:1]
        spread = seconds[0:1, :] + count * jnp.sum(gaps * gaps, axis=0, keepdims=True)
        second = exact(jnp.broadcast_to(spread, eight.shape), to_groups)
        both = jnp.concatenate([mean[0:1], second[0:1]], axis=0)
        out_ref[...] = jnp.broadcast_to(both[None], out_ref.shape)


BLOCKS = 6


def local_stats(bits, field, cot):
    rows, width = field.shape
    block = rows // BLOCKS
    field = pltpu.with_memory_space_constraint(field, pltpu.HBM)
    return pl.pallas_call(
        stats_kernel,
        grid=(BLOCKS // 2,),
        in_specs=[
            IN_SMEM,
            pl.BlockSpec((block, width), lambda i: (2 * i, 0)),
            pl.BlockSpec((block, width), lambda i: (2 * i + 1, 0)),
            pl.BlockSpec((FRAME, width), lambda i: (0, 0)),
            pl.BlockSpec((FRAME, width), lambda i: (rows // FRAME - 1, 0)),
        ],
        out_specs=[
            pl.BlockSpec((64, 2, 128), lambda i: (0, 0, 0)),
            pl.BlockSpec((FRAME, width), lambda i: (0, 0)),
            pl.BlockSpec((FRAME, width), lambda i: (0, 0)),
        ],
        out_shape=[
            jax.ShapeDtypeStruct((64, 2, 128), f32),
            pltpu.HBM((FRAME, width), bf16),
            pltpu.HBM((FRAME, width), bf16),
        ],
        scratch_shapes=[
            pltpu.VMEM((8, width), f32),
            pltpu.VMEM((8, width), f32),
        ],
        compiler_params=params(16),
        cost_estimate=cost(rows * width * 4, rows * width * 2),
    )(bits, field, field, *in_hbm(cot, cot))


def turn_kernel(field_ref, turned_ref):
    turned_ref[...] = field_ref[...].T


def turned(field):
    rows, width = field.shape
    return pl.pallas_call(
        turn_kernel,
        grid=(width // 128,),
        in_specs=[pl.BlockSpec((rows, 128), lambda i: (0, i))],
        out_specs=pl.BlockSpec((128, rows), lambda i: (i, 0)),
        out_shape=pltpu.HBM((width, rows), bf16),
        compiler_params=params(12),
        cost_estimate=cost(10**9, 10**7),
    )(field)


def grad_act_kernel(prev_ref, cur_ref, next_ref, kernel_ref, out_ref):
    out_ref[...] = frame_grad_act(prev_ref[...], cur_ref[...], next_ref[...], kernel_ref)


def frame_grad_act(before, here, after, kernel_ref):
    rows_by_rows = (((1,), (1,)), ((), ()))
    out = lax.dot_general(after, kernel_ref[0], rows_by_rows, preferred_element_type=f32)
    out += lax.dot_general(here, kernel_ref[1], rows_by_rows, preferred_element_type=f32)
    return out + lax.dot_general(before, kernel_ref[2], rows_by_rows, preferred_element_type=f32)


def inner_grad_act(cot, kernel):
    width = cot.shape[1]

    def part(at):
        return pl.BlockSpec((FRAME, width), lambda i: (i + at, 0))

    return pl.pallas_call(
        grad_act_kernel,
        grid=(2,),
        in_specs=[part(0), part(1), part(2), pl.BlockSpec(kernel.shape, lambda i: (0, 0, 0))],
        out_specs=pl.BlockSpec((FRAME, width), lambda i: (i, 0)),
        out_shape=pltpu.HBM((2 * FRAME, width), f32),
        compiler_params=params(20),
        cost_estimate=cost(10**9, 10**7),
    )(*in_hbm(cot, cot, cot, kernel))


def owners(chain):
    out = []
    for block in range(64):
        bit = {name: (block >> (5 - i)) & 1 for i, name in enumerate(OWNER)}
        if bit["z2"] == chain:
            place = 0
            for name in ORDERS[chain]:
                place = 2 * place + bit[name]
            out.append((block, place))
    return out


def segments(chain):
    parts = {}
    for start in range(240 * chain, 1920, 480):
        row = start
        while row < start + 240:
            tap, channel = divmod(row, 640)
            length = min(start + 240 - row, 640 - channel)
            parts.setdefault(tap, []).append((channel, length))
            row += length
    out, at = [], 0
    for tap in sorted(parts):
        out.append((tap, tuple(parts[tap]), at))
        at += sum(length for _, length in parts[tap])
    return out


def add_taps(chain, acc, act_ref, cot_ref, j):
    lanes = slice(CHUNK * j, CHUNK * j + CHUNK)
    for tap, parts, at in segments(chain):
        start = FRAME * (2 - tap) + CHUNK * j
        rows = [act_ref[channel : channel + length, lanes] for channel, length in parts]
        rows = rows[0] if len(rows) == 1 else jnp.concatenate(rows, axis=0)
        part = jnp.dot(rows, cot_ref[start : start + CHUNK, :], preferred_element_type=f32)
        if j == 0:
            acc[at : at + rows.shape[0], :] = part
        else:
            acc[at : at + rows.shape[0], :] += part


def pack_taps(chain, first, acc, send_ref, keep_ref):
    lane = lax.broadcasted_iota(jnp.int32, (32, 128), 1)
    low = lax.broadcasted_iota(jnp.int32, (16, 128), 1)
    for number, (_, place) in enumerate(owners(chain)):
        rows = slice(30 * number, 30 * number + 32)
        tile = [acc[rows, 128 * q : 128 * q + 128] for q in range(5)]
        main = [
            tile[0],
            jnp.where(lane < 96, pltpu.roll(tile[1], 96, 1), pltpu.roll(tile[2], 96, 1)),
            jnp.where(lane < 64, pltpu.roll(tile[2], 64, 1), pltpu.roll(tile[3], 64, 1)),
            jnp.where(lane < 32, pltpu.roll(tile[3], 32, 1), pltpu.roll(tile[4], 32, 1)),
        ]
        rest = [(tile[1], 0), (tile[2], 32), (tile[3], 64), (tile[4], 96)]
        last = []
        for core in range(2):
            pieces = [rest[core], rest[core + 2]]
            row16 = None
            for slot in range(4):
                source, at = pieces[slot % 2]
                part = source[16 * (slot // 2) : 16 * (slot // 2) + 16]
                shift = (32 * slot - at) % 128
                part = part if shift == 0 else pltpu.roll(part, shift, 1)
                row16 = part if row16 is None else jnp.where(low < 32 * slot, row16, part)
            last.append(row16)
        for at, zero, one in ((0, main[0], main[1]), (32, main[2], main[3]), (64, last[0], last[1])):
            span = slice(at, at + zero.shape[0])
            keep_ref[place, span] = jnp.where(first, zero, one)
            send_ref[place, span] = jnp.where(first, one, zero).astype(bf16)


def taps_a_kernel(
    core_ref, stats_ref, gain_ref, field_ref, before_ref, cot_ref, after_ref, tie_ref,
    coef_ref, act_ref, padded_ref, send_ref, keep_ref, acc, wide, field, sems,
):
    width, rows = field_ref.shape
    chunks = rows // CHUNK
    pieces = []
    for j in range(chunks):
        lanes = pl.ds(CHUNK * j, CHUNK)
        pieces.append((field_ref.at[:, lanes], field.at[:, lanes]))
    pieces.append((before_ref, padded_ref.at[pl.ds(0, FRAME)]))
    for t in range(rows // FRAME):
        pieces.append(
            (cot_ref.at[pl.ds(FRAME * t, FRAME)], padded_ref.at[pl.ds(FRAME * (t + 1), FRAME)])
        )
    pieces.append((after_ref, padded_ref.at[pl.ds(FRAME + rows, FRAME)]))
    copies = [pltpu.make_async_copy(*piece, sems.at[q]) for q, piece in enumerate(pieces)]
    copies[0].start()
    total = jnp.sum(stats_ref[...], axis=0)
    mean = total[0:1] * (1.0 / 64)
    gaps = stats_ref[...] - mean[None]
    squares = jnp.sum(gaps * gaps, axis=0)[0:1]
    second = total[1:2] + squares * (CHAN_TOTAL // 64)
    both = jnp.concatenate([mean, second, jnp.zeros((6, 128), f32)], axis=0)
    spread = exact(both, group_columns(128, 0))
    mean, gamma, beta = spread[0:1], gain_ref[0:1, :], gain_ref[1:2, :]
    inv = lax.rsqrt(spread[1:2] * (1.0 / CHAN_TOTAL) + 1e-05)
    coef_ref[...] = jnp.concatenate([mean, inv, gamma, beta, jnp.zeros((4, width), f32)], axis=0)
    scaled = [mean, 0.5 * inv * gamma, 0.5 * beta, jnp.zeros((5, width), f32)]
    coef = jnp.concatenate(scaled, axis=0).T
    for q in range(3):
        wide[q] = jnp.broadcast_to(coef[:, q : q + 1], (width, 128))

    copies[0].wait()
    for q in [1] + list(range(chunks, len(copies) - 2)) + list(range(2, chunks)):
        copies[q].start()
    for copy in copies[-2:]:
        copy.start()

    def activate(j):
        if j == 1:
            copies[j].wait()
        for at in range(CHUNK * j, CHUNK * j + CHUNK, 128):
            lanes = slice(at, at + 128)
            half_normed = (field[:, lanes].astype(f32) - wide[0]) * wide[1] + wide[2]
            act_ref[:, lanes] = (half_normed + half_normed * jnp.tanh(half_normed)).astype(bf16)

    activate(0)
    activate(1)
    needed = chunks + (2 * FRAME + CHUNK - 1) // FRAME + 1
    for copy in copies[chunks:needed]:
        copy.wait()
    add_taps(0, acc, act_ref, padded_ref, 0)
    for copy in copies[needed:] + copies[2:chunks]:
        copy.wait()
    for j in range(1, chunks):
        if j + 1 < chunks:
            activate(j + 1)
        add_taps(0, acc, act_ref, padded_ref, j)
    acc[960:, :] = jnp.zeros((8, width), f32)
    pack_taps(0, core_ref[0] == 0, acc, send_ref, keep_ref)


def taps_a(core, stats, gain, field_t, before, cot, after, tie):
    width, rows = field_t.shape
    return pl.pallas_call(
        taps_a_kernel,
        in_specs=[IN_SMEM] + [IN_VMEM] * 2 + [ANYWHERE] * 5,
        out_specs=[IN_VMEM] * 5,
        out_shape=[
            jax.ShapeDtypeStruct((8, width), f32),
            vmem((width, rows), bf16),
            vmem((rows + 2 * FRAME, width), bf16),
            jax.ShapeDtypeStruct((32, 80, 128), bf16),
            vmem((32, 80, 128), f32),
        ],
        scratch_shapes=[
            pltpu.VMEM((968, width), f32),
            pltpu.VMEM((3, width, 128), f32),
            pltpu.VMEM((width, rows), bf16),
            pltpu.SemaphoreType.DMA((rows // CHUNK + rows // FRAME + 2,)),
        ],
        compiler_params=params(20),
        cost_estimate=cost(3 * width * rows * width, 10**7, width * rows),
    )(core, stats, gain, *in_hbm(field_t, before, cot, after, tie))


def taps_b_kernel(core_ref, act_ref, padded_ref, send_ref, keep_ref, acc):
    width, rows = act_ref.shape
    for j in range(rows // CHUNK):
        add_taps(1, acc, act_ref, padded_ref, j)
    acc[960:, :] = jnp.zeros((8, width), f32)
    pack_taps(1, core_ref[0] == 0, acc, send_ref, keep_ref)


def taps_b(core, act, padded):
    width, rows = act.shape
    return pl.pallas_call(
        taps_b_kernel,
        in_specs=[IN_SMEM, IN_VMEM, IN_VMEM],
        out_specs=[IN_VMEM] * 2,
        out_shape=[
            jax.ShapeDtypeStruct((32, 80, 128), bf16),
            vmem((32, 80, 128), f32),
        ],
        scratch_shapes=[pltpu.VMEM((968, width), f32)],
        compiler_params=params(16),
        cost_estimate=cost(3 * width * rows * width, 10**7),
    )(core, act, padded)


def merge_kernel(slots, terms, bits_ref, *refs):
    count = len(slots)
    ins, sum_refs, outs = refs[: 2 * count], refs[2 * count : 2 * count + terms], refs[2 * count + terms :]
    for q, slot in enumerate(slots):
        kept_ref, got_ref = ins[2 * q : 2 * q + 2]
        keep_ref, send_ref = outs[2 * q : 2 * q + 2]
        size = keep_ref.shape[0]
        mine, other = pl.ds(bits_ref[slot] * size, size), pl.ds((1 - bits_ref[slot]) * size, size)
        keep_ref[...] = kept_ref[mine] + got_ref[mine].astype(f32)
        send_ref[...] = (kept_ref[other] + got_ref[other].astype(f32)).astype(bf16)
    sums_ref = outs[2 * count]
    if terms == 1:
        sums_ref[...] = sum_refs[0][...]
    else:
        every = lax.broadcasted_iota(jnp.int32, sums_ref.shape, 0) < 15
        here, core, there, both = (ref[...] for ref in sum_refs)
        sums_ref[...] = (here + jnp.where(every, core, 0.0)) + (there + jnp.where(every, both, 0.0))


def merge(bits, chains, sums):
    shapes, args = [], []
    for _, kept, got in chains:
        half_shape = (kept.shape[0] // 2,) + kept.shape[1:]
        shapes += [vmem(half_shape, f32), jax.ShapeDtypeStruct(half_shape, bf16)]
        args += [kept, got]
    shapes.append(jax.ShapeDtypeStruct(sums[0].shape, f32))
    args += sums
    slots = [list(BIT).index(bit) for bit, _, _ in chains]
    out = pl.pallas_call(
        functools.partial(merge_kernel, slots, len(sums)),
        in_specs=[IN_SMEM] + [IN_VMEM] * len(args),
        out_specs=[IN_VMEM] * len(shapes),
        out_shape=shapes,
        compiler_params=params(12),
        cost_estimate=cost(10**5, 10**5),
    )(bits, *args)
    return [(out[2 * q], out[2 * q + 1]) for q in range(len(chains))], out[-1]


PART = FRAME


def gradient_kernel(
    inner, tie_ref, field_ref, padded_ref, kernel_ref, coef_ref, held_ref,
    out_ref, field_out_ref, held_out_ref, sums_ref, sums,
):
    step, last = pl.program_id(0), pl.num_programs(0) - 1
    mean, inv, gamma, beta = (coef_ref[q : q + 1, :] for q in range(4))

    @pl.when(step == 0)
    def _():
        sums[...] = held_ref[...]

    frame = 1 + step if inner else 3 * step
    for part in range(0, FRAME, PART):
        near = [
            padded_ref[pl.ds(pl.multiple_of((frame + t) * FRAME + part, 16), PART), :]
            for t in ((1,) if inner else (0, 1, 2))
        ]
        cot = near[len(near) // 2].astype(f32)
        grad = kernel_ref[part : part + PART, :] if inner else frame_grad_act(*near, kernel_ref)
        field = field_ref[part : part + PART, :]
        unit = (field.astype(f32) - mean) * inv
        half_normed = unit * (0.5 * gamma) + 0.5 * beta
        turn = jnp.tanh(half_normed)
        grad = grad * (0.5 * ((1.0 + turn) + half_normed * (1.0 - turn * turn)))
        rows = pl.ds(pl.multiple_of(step * FRAME + part, 16), PART)
        out_ref[rows, :] = cot + (inv * gamma) * grad
        field_out_ref[rows, :] = field
        sums[0:1, :] += jnp.sum(grad, axis=0, keepdims=True)
        sums[1:2, :] += jnp.sum(grad * unit, axis=0, keepdims=True)
        sums[2:3, :] += jnp.sum(cot, axis=0, keepdims=True)

    @pl.when(step == last)
    def _():
        held_out_ref[...] = sums[...]
        for q in range(3):
            for at in range(5):
                sums_ref[5 * q + at : 5 * q + at + 1, :] = sums[q : q + 1, 128 * at : 128 * at + 128]
        weighted = sums[...] * gamma
        sums_ref[15:16, :] = (
            exact(weighted, group_rows(128, 0))[0:1] + exact(weighted, group_rows(128, GROUPS))[1:2]
        )


def gradient(tie, inner, field, padded, kernel, coef, held):
    width = field.shape[1]

    top = pl.BlockSpec((8, width), lambda i: (0, 0))
    return pl.pallas_call(
        functools.partial(gradient_kernel, inner),
        grid=(2,),
        in_specs=[
            ANYWHERE,
            pl.BlockSpec((FRAME, width), lambda i: (1 + i if inner else 3 * i, 0)),
            IN_VMEM,
            pl.BlockSpec((FRAME, width), lambda i: (i, 0)) if inner else IN_VMEM,
            top,
            top,
        ],
        out_specs=[
            IN_VMEM,
            IN_VMEM,
            top,
            pl.BlockSpec((16, 128), lambda i: (0, 0)),
        ],
        out_shape=[
            vmem((2 * FRAME, width), f32),
            vmem((2 * FRAME, width), bf16),
            jax.ShapeDtypeStruct((8, width), f32),
            jax.ShapeDtypeStruct((16, 128), f32),
        ],
        scratch_shapes=[pltpu.VMEM((8, width), f32)],
        compiler_params=params(16),
        cost_estimate=cost(1, 1),
    )(tie, field, padded, kernel, coef, held)


def result_kernel(inner_ref, outer_ref, inner_field_ref, outer_field_ref, coef_ref, sums_ref, out_ref, means):
    @pl.when(pl.program_id(0) == 0)
    def _():
        grouped = jnp.broadcast_to(sums_ref[15:16, :], (8, 128)) * (1.0 / CHAN_TOTAL)
        means[0:1, :] = exact(grouped, group_columns(128, 0))[0:1]
        means[1:2, :] = exact(grouped, group_columns(128, GROUPS))[0:1]

    size, step = out_ref.shape[0], pl.program_id(0)
    per_frame = FRAME // size
    inner = (step >= per_frame) & (step < 3 * per_frame)
    before = jnp.where(inner, per_frame, jnp.where(step < per_frame, 0, 2 * per_frame))
    rows = pl.ds(pl.multiple_of((step - before) * size, size), size)
    mean, inv = coef_ref[0:1, :], coef_ref[1:2, :]
    choices = (
        (inner, inner_ref, inner_field_ref),
        (jnp.logical_not(inner), outer_ref, outer_field_ref),
    )
    for when, grad_ref, field_ref in choices:

        @pl.when(when)
        def _():
            unit = (field_ref[rows, :].astype(f32) - mean) * inv
            taken = inv * (means[0:1, :] + unit * means[1:2, :])
            out_ref[...] = (grad_ref[rows, :] - taken).astype(bf16)


def grad_of_field(inner, outer, inner_field, outer_field, coef, sums, block=288):
    rows, width = 2 * inner.shape[0], inner.shape[1]
    tile = pl.BlockSpec((block, width), lambda i: (i, 0))
    return pl.pallas_call(
        result_kernel,
        grid=(rows // block,),
        in_specs=[
            IN_VMEM,
            IN_VMEM,
            IN_VMEM,
            IN_VMEM,
            pl.BlockSpec((8, width), lambda i: (0, 0)),
            pl.BlockSpec((16, 128), lambda i: (0, 0)),
        ],
        out_specs=tile,
        out_shape=jax.ShapeDtypeStruct((rows, width), bf16),
        scratch_shapes=[pltpu.VMEM((8, width), f32)],
        compiler_params=params(12),
        cost_estimate=cost(rows * width * 9, rows * width * 10),
    )(inner, outer, inner_field, outer_field, coef, sums)


def per_device(field, cotangent, gamma, beta, kernel):
    _, frames, rows, cells, width = field.shape
    loss_scale = 1.0 / math.sqrt(4 * 128 * 18 * 64)
    place = lax.axis_index(AXES)
    own = {name: (place >> bit) & 1 for name, bit in BIT.items()}
    off = {name: 1 - bit for name, bit in own.items()}
    bits = jnp.stack(list(own.values()) + list(off.values())).astype(jnp.int32)
    core = own["core"].astype(jnp.int32).reshape(1)
    gain = jnp.concatenate([gamma[None], beta[None], jnp.zeros((6, width), f32)], axis=0)

    flat, cot = field.reshape(-1, width), cotangent.reshape(-1, width)
    stats, first, final = local_stats(bits, flat, cot)
    up = [(i, i + 1) for i in range(31)]
    before = lax.ppermute(final, "tm", up)
    after = lax.ppermute(first, "tm", [(j, i) for i, j in up])
    stats = lax.all_to_all(stats, ("tm", "height"), 0, 0)
    field_t = turned(flat)
    grad_inner = inner_grad_act(cot, kernel)

    coef, act_t, padded, send_a, keep_a = taps_a(
        core, stats, gain, field_t, before, cot, after, grad_inner
    )
    got_a = swap(send_a, "core")
    send_b, keep_b = taps_b(core, act_t, padded)
    got_b = swap(send_b, "core")
    none = jnp.zeros((8, width), f32)
    inner, inner_field, held, _ = gradient(keep_b, True, flat, padded, grad_inner, coef, none)
    kept, got = [keep_a, keep_b], [got_a, got_b]
    sums = [held]
    for step in range(3):
        merged, sums = merge(bits, [(ORDERS[q][step], kept[q], got[q]) for q in range(2)], sums)
        kept = [merged[q][0] for q in range(2)]
        got = [
            lax.ppermute(merged[q][1], AXES, neighbours(NEAR[ORDERS[q][step]])) for q in range(2)
        ]
        if step == 0:
            outer, outer_field, _, sums = gradient(kept[0], False, flat, padded, kernel, coef, sums)
            sums = [sums]
        elif step == 1:
            sums = [sums, swap(sums, "core"), swap(sums, "z0"), swap(sums, "core", "z0")]
        else:
            sums = (sums + swap(sums, "x0")) + (swap(sums, "yl") + swap(sums, "x0", "yl"))
    taps = jnp.stack([kept[q] + got[q].astype(f32) for q in range(2)])
    taps = taps.reshape(2, 2, 2, 80, 128)
    taps, sums = far_halve(taps, 2, "z1", own, off, sums)
    taps, sums = far_halve(taps, 1, "x1", own, off, sums)
    taps, sums = far_halve(taps, 0, "z2", own, off, sums)
    field_grad = grad_of_field(inner, outer, inner_field, outer_field, coef, sums)

    got, sums = far_swap(taps, sums, "yh")
    taps = taps + got
    main = half(taps[:64].reshape(2, 32, 128), 0, own["yh"])
    rest = half(taps[64:].reshape(16, 2, 2, 32), 2, own["yh"])
    rest = jnp.concatenate([rest[:, 0], rest[:, 1]], axis=0)
    kernel_grad = jnp.concatenate([main, rest], axis=1)[:30] * loss_scale
    channel_grads = sums[:15].reshape(3, width) * loss_scale
    return (field_grad.reshape(field.shape), kernel_grad, channel_grads)


def solution(mesh):
    spread = P("dp", "tm", "height", None, None)
    return jax.shard_map(
        per_device,
        mesh=mesh,
        in_specs=(spread, spread, P(), P(), P()),
        out_specs=(spread, P(("tm", "height"), "dp"), P()),
        check_vma=False,
    )
```

```python
import functools
import math

import jax
import jax.numpy as jnp
from jax import lax
from jax.experimental import pallas as pl
from jax.experimental.pallas import tpu as pltpu
from jax.sharding import PartitionSpec as P

GROUPS = 32
CPG = 20
FRAME = 576
CHUNK = 768
CHAN_TOTAL = 128 * 18 * 64 * CPG
AXES = ("dp", "tm", "height")
BIT = {"yh": 7, "core": 6, "x1": 5, "x0": 4, "z2": 3, "z1": 2, "z0": 1, "yl": 0}
OWNER = ("x1", "x0", "z2", "z1", "z0", "yl")
ORDERS = (("z0", "x0", "yl", "x1", "z1"), ("yl", "z0", "x0", "x1", "z1"))
f32 = jnp.float32
bf16 = jnp.bfloat16
IN_VMEM = pl.BlockSpec(memory_space=pltpu.VMEM)
ANYWHERE = pl.BlockSpec(memory_space=pl.ANY)
IN_SMEM = pl.BlockSpec(memory_space=pltpu.SMEM)


def params(mib):
    return pltpu.CompilerParams(vmem_limit_bytes=mib * 2**20)


def vmem(shape, dtype):
    return pltpu.VMEM(shape, dtype)


def in_hbm(*arrays):
    return [pltpu.with_memory_space_constraint(array, pltpu.HBM) for array in arrays]


def cost(flops, moved, transcendentals=0):
    return pl.CostEstimate(flops=flops, bytes_accessed=moved, transcendentals=transcendentals)


def pairs(bits):
    mask = sum(1 << BIT[bit] for bit in bits)
    return [(i, i ^ mask) for i in range(256)]


def neighbours(axis):
    out = []
    for i in range(256):
        bit = {name: (i >> at) & 1 for name, at in BIT.items()}
        x, y = 2 * bit["x1"] + bit["x0"], 2 * bit["yh"] + bit["yl"]
        z = 4 * bit["z2"] + 2 * bit["z1"] + bit["z0"]
        place = {"x": x, "y": y, "z": z}
        size = 8 if axis == "z" else 4
        at = place[axis]
        step = 1 if (at % 2 == 0) == (bit["core"] == 0) else -1
        place[axis] = (at + step) % size
        x, y, z = place["x"], place["y"], place["z"]
        out.append((i, (((y >> 1) * 2 + bit["core"]) * 32 + x * 8 + z) * 2 + (y & 1)))
    return out


NEAR = {"z0": "z", "x0": "x", "yl": "y"}


def swap(value, *bits):
    chosen = pairs(bits)
    if bits == ("z1",):
        both = pairs(("z1", "z2"))
        chosen = [both[i] if (i >> BIT["core"]) & 1 else pair for i, pair in enumerate(chosen)]
    return lax.ppermute(value, AXES, chosen)


def half(total, axis, index):
    return lax.dynamic_index_in_dim(total, index, axis, False, allow_negative_indices=False)


def far_swap(send, sums, bit):
    high = lax.reduce_precision(sums, 8, 7)
    rest = sums - high
    middle = lax.reduce_precision(rest, 8, 7)
    parts = [part.astype(bf16) for part in (high, middle, rest - middle)]
    rows = send.reshape(-1, 128)
    got = swap(jnp.concatenate([rows.astype(bf16)] + parts, axis=0), bit).astype(f32)
    cut, count = rows.shape[0], sums.shape[0]
    other = [got[cut + i * count : cut + (i + 1) * count] for i in range(3)]
    return got[:cut].reshape(send.shape), sums + (other[0] + (other[1] + other[2]))


def far_halve(total, axis, bit, own, off, sums):
    keep = half(total, axis, own[bit])
    send = half(total, axis, off[bit])
    got, sums = far_swap(send, sums, bit)
    return keep + got, sums


def group_rows(lanes, first):
    channel = lax.broadcasted_iota(jnp.int32, (640, lanes), 0)
    start = (lax.broadcasted_iota(jnp.int32, (640, lanes), 1) - first) * CPG
    return jnp.where((channel >= start) & (channel < start + CPG), 1.0, 0.0).astype(f32)


def group_columns(rows, first):
    channel = lax.broadcasted_iota(jnp.int32, (rows, 640), 1)
    start = (lax.broadcasted_iota(jnp.int32, (rows, 640), 0) - first) * CPG
    return jnp.where((channel >= start) & (channel < start + CPG), 1.0, 0.0).astype(f32)


def exact(left, right):
    return jnp.dot(left, right, preferred_element_type=f32, precision=lax.Precision.HIGHEST)


def stats_kernel(
    bits_ref, upper_ref, lower_ref, head_ref, tail_ref, out_ref, first_ref, final_ref, means, seconds
):
    step, last = pl.program_id(0), pl.num_programs(0) - 1
    count = upper_ref.shape[0]
    @pl.when(step == 0)
    def _():
        first_ref[...] = head_ref[...]
        final_ref[...] = tail_ref[...]
        means[...] = jnp.zeros_like(means)
        seconds[...] = jnp.zeros_like(seconds)

    for part, ref in enumerate((upper_ref, lower_ref)):
        mean = jnp.sum(ref[...].astype(f32), axis=0, keepdims=True) * (1.0 / count)
        gap = ref[...].astype(f32) - mean
        means[pl.ds(2 * step + part, 1), :] = mean
        seconds[0:1, :] += jnp.sum(gap * gap, axis=0, keepdims=True)

    @pl.when(step == last)
    def _():
        blocks = BLOCKS
        total = jnp.sum(means[...], axis=0, keepdims=True) * (1.0 / blocks)
        to_groups, to_channels = group_rows(128, 0), group_columns(128, 0)
        eight = jnp.broadcast_to(total, (8, total.shape[1]))
        mean = exact(eight, to_groups) * (1.0 / CPG)
        gaps = means[0:blocks, :] - exact(mean, to_channels)[0:1]
        spread = seconds[0:1, :] + count * jnp.sum(gaps * gaps, axis=0, keepdims=True)
        second = exact(jnp.broadcast_to(spread, eight.shape), to_groups)
        both = jnp.concatenate([mean[0:1], second[0:1]], axis=0)
        out_ref[...] = jnp.broadcast_to(both[None], out_ref.shape)


BLOCKS = 6


def local_stats(bits, field, cot):
    rows, width = field.shape
    block = rows // BLOCKS
    field = pltpu.with_memory_space_constraint(field, pltpu.HBM)
    return pl.pallas_call(
        stats_kernel,
        grid=(BLOCKS // 2,),
        in_specs=[
            IN_SMEM,
            pl.BlockSpec((block, width), lambda i: (2 * i, 0)),
            pl.BlockSpec((block, width), lambda i: (2 * i + 1, 0)),
            pl.BlockSpec((FRAME, width), lambda i: (0, 0)),
            pl.BlockSpec((FRAME, width), lambda i: (rows // FRAME - 1, 0)),
        ],
        out_specs=[
            pl.BlockSpec((64, 2, 128), lambda i: (0, 0, 0)),
            pl.BlockSpec((FRAME, width), lambda i: (0, 0)),
            pl.BlockSpec((FRAME, width), lambda i: (0, 0)),
        ],
        out_shape=[
            jax.ShapeDtypeStruct((64, 2, 128), f32),
            pltpu.HBM((FRAME, width), bf16),
            pltpu.HBM((FRAME, width), bf16),
        ],
        scratch_shapes=[
            pltpu.VMEM((8, width), f32),
            pltpu.VMEM((8, width), f32),
        ],
        compiler_params=params(16),
        cost_estimate=cost(rows * width * 4, rows * width * 2),
    )(bits, field, field, *in_hbm(cot, cot))


def turn_kernel(field_ref, turned_ref):
    turned_ref[...] = field_ref[...].T


def turned(field):
    rows, width = field.shape
    return pl.pallas_call(
        turn_kernel,
        grid=(width // 128,),
        in_specs=[pl.BlockSpec((rows, 128), lambda i: (0, i))],
        out_specs=pl.BlockSpec((128, rows), lambda i: (i, 0)),
        out_shape=pltpu.HBM((width, rows), bf16),
        compiler_params=params(12),
        cost_estimate=cost(10**9, 10**7),
    )(field)


def grad_act_kernel(prev_ref, cur_ref, next_ref, kernel_ref, out_ref):
    out_ref[...] = frame_grad_act(prev_ref[...], cur_ref[...], next_ref[...], kernel_ref)


def frame_grad_act(before, here, after, kernel_ref):
    rows_by_rows = (((1,), (1,)), ((), ()))
    out = lax.dot_general(after, kernel_ref[0], rows_by_rows, preferred_element_type=f32)
    out += lax.dot_general(here, kernel_ref[1], rows_by_rows, preferred_element_type=f32)
    return out + lax.dot_general(before, kernel_ref[2], rows_by_rows, preferred_element_type=f32)


def inner_grad_act(cot, kernel):
    width = cot.shape[1]

    def part(at):
        return pl.BlockSpec((FRAME, width), lambda i: (i + at, 0))

    return pl.pallas_call(
        grad_act_kernel,
        grid=(2,),
        in_specs=[part(0), part(1), part(2), pl.BlockSpec(kernel.shape, lambda i: (0, 0, 0))],
        out_specs=pl.BlockSpec((FRAME, width), lambda i: (i, 0)),
        out_shape=pltpu.HBM((2 * FRAME, width), f32),
        compiler_params=params(20),
        cost_estimate=cost(10**9, 10**7),
    )(*in_hbm(cot, cot, cot, kernel))


def owners(chain):
    out = []
    for block in range(64):
        bit = {name: (block >> (5 - i)) & 1 for i, name in enumerate(OWNER)}
        if bit["z2"] == chain:
            place = 0
            for name in ORDERS[chain]:
                place = 2 * place + bit[name]
            out.append((block, place))
    return out


def segments(chain):
    parts = {}
    for start in range(240 * chain, 1920, 480):
        row = start
        while row < start + 240:
            tap, channel = divmod(row, 640)
            length = min(start + 240 - row, 640 - channel)
            parts.setdefault(tap, []).append((channel, length))
            row += length
    out, at = [], 0
    for tap in sorted(parts):
        out.append((tap, tuple(parts[tap]), at))
        at += sum(length for _, length in parts[tap])
    return out


def add_taps(chain, acc, act_ref, cot_ref, j):
    lanes = slice(CHUNK * j, CHUNK * j + CHUNK)
    for tap, parts, at in segments(chain):
        start = FRAME * (2 - tap) + CHUNK * j
        rows = [act_ref[channel : channel + length, lanes] for channel, length in parts]
        rows = rows[0] if len(rows) == 1 else jnp.concatenate(rows, axis=0)
        part = jnp.dot(rows, cot_ref[start : start + CHUNK, :], preferred_element_type=f32)
        if j == 0:
            acc[at : at + rows.shape[0], :] = part
        else:
            acc[at : at + rows.shape[0], :] += part


def pack_taps(chain, first, acc, send_ref, keep_ref):
    lane = lax.broadcasted_iota(jnp.int32, (32, 128), 1)
    low = lax.broadcasted_iota(jnp.int32, (16, 128), 1)
    for number, (_, place) in enumerate(owners(chain)):
        rows = slice(30 * number, 30 * number + 32)
        tile = [acc[rows, 128 * q : 128 * q + 128] for q in range(5)]
        main = [
            tile[0],
            jnp.where(lane < 96, pltpu.roll(tile[1], 96, 1), pltpu.roll(tile[2], 96, 1)),
            jnp.where(lane < 64, pltpu.roll(tile[2], 64, 1), pltpu.roll(tile[3], 64, 1)),
            jnp.where(lane < 32, pltpu.roll(tile[3], 32, 1), pltpu.roll(tile[4], 32, 1)),
        ]
        rest = [(tile[1], 0), (tile[2], 32), (tile[3], 64), (tile[4], 96)]
        last = []
        for core in range(2):
            pieces = [rest[core], rest[core + 2]]
            row16 = None
            for slot in range(4):
                source, at = pieces[slot % 2]
                part = source[16 * (slot // 2) : 16 * (slot // 2) + 16]
                shift = (32 * slot - at) % 128
                part = part if shift == 0 else pltpu.roll(part, shift, 1)
                row16 = part if row16 is None else jnp.where(low < 32 * slot, row16, part)
            last.append(row16)
        for at, zero, one in ((0, main[0], main[1]), (32, main[2], main[3]), (64, last[0], last[1])):
            span = slice(at, at + zero.shape[0])
            keep_ref[place, span] = jnp.where(first, zero, one)
            send_ref[place, span] = jnp.where(first, one, zero).astype(bf16)


def taps_a_kernel(
    core_ref, stats_ref, gain_ref, field_ref, before_ref, cot_ref, after_ref, tie_ref,
    coef_ref, act_ref, padded_ref, send_ref, keep_ref, acc, wide, field, sems,
):
    width, rows = field_ref.shape
    chunks = rows // CHUNK
    pieces = []
    for j in range(chunks):
        lanes = pl.ds(CHUNK * j, CHUNK)
        pieces.append((field_ref.at[:, lanes], field.at[:, lanes]))
    pieces.append((before_ref, padded_ref.at[pl.ds(0, FRAME)]))
    for t in range(rows // FRAME):
        pieces.append(
            (cot_ref.at[pl.ds(FRAME * t, FRAME)], padded_ref.at[pl.ds(FRAME * (t + 1), FRAME)])
        )
    pieces.append((after_ref, padded_ref.at[pl.ds(FRAME + rows, FRAME)]))
    copies = [pltpu.make_async_copy(*piece, sems.at[q]) for q, piece in enumerate(pieces)]
    for q in [0, 1] + list(range(chunks, len(copies) - 2)) + list(range(2, chunks)):
        copies[q].start()
    for copy in copies[-2:]:
        copy.start()
    total = jnp.sum(stats_ref[...], axis=0)
    mean = total[0:1] * (1.0 / 64)
    gaps = stats_ref[...] - mean[None]
    squares = jnp.sum(gaps * gaps, axis=0)[0:1]
    second = total[1:2] + squares * (CHAN_TOTAL // 64)
    both = jnp.concatenate([mean, second, jnp.zeros((6, 128), f32)], axis=0)
    spread = exact(both, group_columns(128, 0))
    mean, gamma, beta = spread[0:1], gain_ref[0:1, :], gain_ref[1:2, :]
    inv = lax.rsqrt(spread[1:2] * (1.0 / CHAN_TOTAL) + 1e-05)
    coef_ref[...] = jnp.concatenate([mean, inv, gamma, beta, jnp.zeros((4, width), f32)], axis=0)
    scaled = [mean, 0.5 * inv * gamma, 0.5 * beta, jnp.zeros((5, width), f32)]
    coef = jnp.concatenate(scaled, axis=0).T
    for q in range(3):
        wide[q] = jnp.broadcast_to(coef[:, q : q + 1], (width, 128))

    copies[0].wait()

    def activate(j):
        if j == 1:
            copies[j].wait()
        for at in range(CHUNK * j, CHUNK * j + CHUNK, 128):
            lanes = slice(at, at + 128)
            half_normed = (field[:, lanes].astype(f32) - wide[0]) * wide[1] + wide[2]
            act_ref[:, lanes] = (half_normed + half_normed * jnp.tanh(half_normed)).astype(bf16)

    activate(0)
    activate(1)
    needed = chunks + (2 * FRAME + CHUNK - 1) // FRAME + 1
    for copy in copies[chunks:needed]:
        copy.wait()
    add_taps(0, acc, act_ref, padded_ref, 0)
    for copy in copies[needed:] + copies[2:chunks]:
        copy.wait()
    for j in range(1, chunks):
        if j + 1 < chunks:
            activate(j + 1)
        add_taps(0, acc, act_ref, padded_ref, j)
    acc[960:, :] = jnp.zeros((8, width), f32)
    pack_taps(0, core_ref[0] == 0, acc, send_ref, keep_ref)


def taps_a(core, stats, gain, field_t, before, cot, after, tie):
    width, rows = field_t.shape
    return pl.pallas_call(
        taps_a_kernel,
        in_specs=[IN_SMEM] + [IN_VMEM] * 2 + [ANYWHERE] * 5,
        out_specs=[IN_VMEM] * 5,
        out_shape=[
            jax.ShapeDtypeStruct((8, width), f32),
            vmem((width, rows), bf16),
            vmem((rows + 2 * FRAME, width), bf16),
            jax.ShapeDtypeStruct((32, 80, 128), bf16),
            vmem((32, 80, 128), f32),
        ],
        scratch_shapes=[
            pltpu.VMEM((968, width), f32),
            pltpu.VMEM((3, width, 128), f32),
            pltpu.VMEM((width, rows), bf16),
            pltpu.SemaphoreType.DMA((rows // CHUNK + rows // FRAME + 2,)),
        ],
        compiler_params=params(20),
        cost_estimate=cost(3 * width * rows * width, 10**7, width * rows),
    )(core, stats, gain, *in_hbm(field_t, before, cot, after, tie))


def taps_b_kernel(core_ref, act_ref, padded_ref, send_ref, keep_ref, acc):
    width, rows = act_ref.shape
    for j in range(rows // CHUNK):
        add_taps(1, acc, act_ref, padded_ref, j)
    acc[960:, :] = jnp.zeros((8, width), f32)
    pack_taps(1, core_ref[0] == 0, acc, send_ref, keep_ref)


def taps_b(core, act, padded):
    width, rows = act.shape
    return pl.pallas_call(
        taps_b_kernel,
        in_specs=[IN_SMEM, IN_VMEM, IN_VMEM],
        out_specs=[IN_VMEM] * 2,
        out_shape=[
            jax.ShapeDtypeStruct((32, 80, 128), bf16),
            vmem((32, 80, 128), f32),
        ],
        scratch_shapes=[pltpu.VMEM((968, width), f32)],
        compiler_params=params(16),
        cost_estimate=cost(3 * width * rows * width, 10**7),
    )(core, act, padded)


def merge_kernel(slots, terms, bits_ref, *refs):
    count = len(slots)
    ins, sum_refs, outs = refs[: 2 * count], refs[2 * count : 2 * count + terms], refs[2 * count + terms :]
    for q, slot in enumerate(slots):
        kept_ref, got_ref = ins[2 * q : 2 * q + 2]
        keep_ref, send_ref = outs[2 * q : 2 * q + 2]
        size = keep_ref.shape[0]
        mine, other = pl.ds(bits_ref[slot] * size, size), pl.ds((1 - bits_ref[slot]) * size, size)
        keep_ref[...] = kept_ref[mine] + got_ref[mine].astype(f32)
        send_ref[...] = (kept_ref[other] + got_ref[other].astype(f32)).astype(bf16)
    sums_ref = outs[2 * count]
    if terms == 1:
        sums_ref[...] = sum_refs[0][...]
    else:
        every = lax.broadcasted_iota(jnp.int32, sums_ref.shape, 0) < 15
        here, core, there, both = (ref[...] for ref in sum_refs)
        sums_ref[...] = (here + jnp.where(every, core, 0.0)) + (there + jnp.where(every, both, 0.0))


def merge(bits, chains, sums):
    shapes, args = [], []
    for _, kept, got in chains:
        half_shape = (kept.shape[0] // 2,) + kept.shape[1:]
        shapes += [vmem(half_shape, f32), jax.ShapeDtypeStruct(half_shape, bf16)]
        args += [kept, got]
    shapes.append(jax.ShapeDtypeStruct(sums[0].shape, f32))
    args += sums
    slots = [list(BIT).index(bit) for bit, _, _ in chains]
    out = pl.pallas_call(
        functools.partial(merge_kernel, slots, len(sums)),
        in_specs=[IN_SMEM] + [IN_VMEM] * len(args),
        out_specs=[IN_VMEM] * len(shapes),
        out_shape=shapes,
        compiler_params=params(12),
        cost_estimate=cost(10**5, 10**5),
    )(bits, *args)
    return [(out[2 * q], out[2 * q + 1]) for q in range(len(chains))], out[-1]


PART = FRAME


def gradient_kernel(
    inner, tie_ref, field_ref, padded_ref, kernel_ref, coef_ref, held_ref,
    out_ref, field_out_ref, held_out_ref, sums_ref, sums,
):
    step, last = pl.program_id(0), pl.num_programs(0) - 1
    mean, inv, gamma, beta = (coef_ref[q : q + 1, :] for q in range(4))

    @pl.when(step == 0)
    def _():
        sums[...] = held_ref[...]

    frame = 1 + step if inner else 3 * step
    for part in range(0, FRAME, PART):
        near = [
            padded_ref[pl.ds(pl.multiple_of((frame + t) * FRAME + part, 16), PART), :]
            for t in ((1,) if inner else (0, 1, 2))
        ]
        cot = near[len(near) // 2].astype(f32)
        grad = kernel_ref[part : part + PART, :] if inner else frame_grad_act(*near, kernel_ref)
        field = field_ref[part : part + PART, :]
        unit = (field.astype(f32) - mean) * inv
        half_normed = unit * (0.5 * gamma) + 0.5 * beta
        turn = jnp.tanh(half_normed)
        grad = grad * (0.5 * ((1.0 + turn) + half_normed * (1.0 - turn * turn)))
        rows = pl.ds(pl.multiple_of(step * FRAME + part, 16), PART)
        out_ref[rows, :] = cot + (inv * gamma) * grad
        field_out_ref[rows, :] = field
        sums[0:1, :] += jnp.sum(grad, axis=0, keepdims=True)
        sums[1:2, :] += jnp.sum(grad * unit, axis=0, keepdims=True)
        sums[2:3, :] += jnp.sum(cot, axis=0, keepdims=True)

    @pl.when(step == last)
    def _():
        held_out_ref[...] = sums[...]
        for q in range(3):
            for at in range(5):
                sums_ref[5 * q + at : 5 * q + at + 1, :] = sums[q : q + 1, 128 * at : 128 * at + 128]
        weighted = sums[...] * gamma
        sums_ref[15:16, :] = (
            exact(weighted, group_rows(128, 0))[0:1] + exact(weighted, group_rows(128, GROUPS))[1:2]
        )


def gradient(tie, inner, field, padded, kernel, coef, held):
    width = field.shape[1]

    top = pl.BlockSpec((8, width), lambda i: (0, 0))
    return pl.pallas_call(
        functools.partial(gradient_kernel, inner),
        grid=(2,),
        in_specs=[
            ANYWHERE,
            pl.BlockSpec((FRAME, width), lambda i: (1 + i if inner else 3 * i, 0)),
            IN_VMEM,
            pl.BlockSpec((FRAME, width), lambda i: (i, 0)) if inner else IN_VMEM,
            top,
            top,
        ],
        out_specs=[
            IN_VMEM,
            IN_VMEM,
            top,
            pl.BlockSpec((16, 128), lambda i: (0, 0)),
        ],
        out_shape=[
            vmem((2 * FRAME, width), f32),
            vmem((2 * FRAME, width), bf16),
            jax.ShapeDtypeStruct((8, width), f32),
            jax.ShapeDtypeStruct((16, 128), f32),
        ],
        scratch_shapes=[pltpu.VMEM((8, width), f32)],
        compiler_params=params(16),
        cost_estimate=cost(1, 1),
    )(tie, field, padded, kernel, coef, held)


def result_kernel(inner_ref, outer_ref, inner_field_ref, outer_field_ref, coef_ref, sums_ref, out_ref, means):
    @pl.when(pl.program_id(0) == 0)
    def _():
        grouped = jnp.broadcast_to(sums_ref[15:16, :], (8, 128)) * (1.0 / CHAN_TOTAL)
        means[0:1, :] = exact(grouped, group_columns(128, 0))[0:1]
        means[1:2, :] = exact(grouped, group_columns(128, GROUPS))[0:1]

    size, step = out_ref.shape[0], pl.program_id(0)
    per_frame = FRAME // size
    inner = (step >= per_frame) & (step < 3 * per_frame)
    before = jnp.where(inner, per_frame, jnp.where(step < per_frame, 0, 2 * per_frame))
    rows = pl.ds(pl.multiple_of((step - before) * size, size), size)
    mean, inv = coef_ref[0:1, :], coef_ref[1:2, :]
    choices = (
        (inner, inner_ref, inner_field_ref),
        (jnp.logical_not(inner), outer_ref, outer_field_ref),
    )
    for when, grad_ref, field_ref in choices:

        @pl.when(when)
        def _():
            unit = (field_ref[rows, :].astype(f32) - mean) * inv
            taken = inv * (means[0:1, :] + unit * means[1:2, :])
            out_ref[...] = (grad_ref[rows, :] - taken).astype(bf16)


def grad_of_field(inner, outer, inner_field, outer_field, coef, sums, block=288):
    rows, width = 2 * inner.shape[0], inner.shape[1]
    tile = pl.BlockSpec((block, width), lambda i: (i, 0))
    return pl.pallas_call(
        result_kernel,
        grid=(rows // block,),
        in_specs=[
            IN_VMEM,
            IN_VMEM,
            IN_VMEM,
            IN_VMEM,
            pl.BlockSpec((8, width), lambda i: (0, 0)),
            pl.BlockSpec((16, 128), lambda i: (0, 0)),
        ],
        out_specs=tile,
        out_shape=jax.ShapeDtypeStruct((rows, width), bf16),
        scratch_shapes=[pltpu.VMEM((8, width), f32)],
        compiler_params=params(12),
        cost_estimate=cost(rows * width * 9, rows * width * 10),
    )(inner, outer, inner_field, outer_field, coef, sums)


def per_device(field, cotangent, gamma, beta, kernel):
    _, frames, rows, cells, width = field.shape
    loss_scale = 1.0 / math.sqrt(4 * 128 * 18 * 64)
    place = lax.axis_index(AXES)
    own = {name: (place >> bit) & 1 for name, bit in BIT.items()}
    off = {name: 1 - bit for name, bit in own.items()}
    bits = jnp.stack(list(own.values()) + list(off.values())).astype(jnp.int32)
    core = own["core"].astype(jnp.int32).reshape(1)
    gain = jnp.concatenate([gamma[None], beta[None], jnp.zeros((6, width), f32)], axis=0)

    flat, cot = field.reshape(-1, width), cotangent.reshape(-1, width)
    stats, first, final = local_stats(bits, flat, cot)
    up = [(i, i + 1) for i in range(31)]
    before = lax.ppermute(final, "tm", up)
    after = lax.ppermute(first, "tm", [(j, i) for i, j in up])
    stats = lax.all_to_all(stats, ("tm", "height"), 0, 0)
    field_t = turned(flat)
    grad_inner = inner_grad_act(cot, kernel)

    coef, act_t, padded, send_a, keep_a = taps_a(
        core, stats, gain, field_t, before, cot, after, grad_inner
    )
    got_a = swap(send_a, "core")
    send_b, keep_b = taps_b(core, act_t, padded)
    got_b = swap(send_b, "core")
    none = jnp.zeros((8, width), f32)
    inner, inner_field, held, _ = gradient(keep_b, True, flat, padded, grad_inner, coef, none)
    kept, got = [keep_a, keep_b], [got_a, got_b]
    sums = [held]
    for step in range(3):
        merged, sums = merge(bits, [(ORDERS[q][step], kept[q], got[q]) for q in range(2)], sums)
        kept = [merged[q][0] for q in range(2)]
        got = [
            lax.ppermute(merged[q][1], AXES, neighbours(NEAR[ORDERS[q][step]])) for q in range(2)
        ]
        if step == 0:
            outer, outer_field, _, sums = gradient(kept[0], False, flat, padded, kernel, coef, sums)
            sums = [sums]
        elif step == 1:
            sums = [sums, swap(sums, "core"), swap(sums, "z0"), swap(sums, "core", "z0")]
        else:
            sums = (sums + swap(sums, "x0")) + (swap(sums, "yl") + swap(sums, "x0", "yl"))
    taps = jnp.stack([kept[q] + got[q].astype(f32) for q in range(2)])
    taps = taps.reshape(2, 2, 2, 80, 128)
    taps, sums = far_halve(taps, 2, "z1", own, off, sums)
    taps, sums = far_halve(taps, 1, "x1", own, off, sums)
    taps, sums = far_halve(taps, 0, "z2", own, off, sums)
    field_grad = grad_of_field(inner, outer, inner_field, outer_field, coef, sums)

    got, sums = far_swap(taps, sums, "yh")
    taps = taps + got
    main = half(taps[:64].reshape(2, 32, 128), 0, own["yh"])
    rest = half(taps[64:].reshape(16, 2, 2, 32), 2, own["yh"])
    rest = jnp.concatenate([rest[:, 0], rest[:, 1]], axis=0)
    kernel_grad = jnp.concatenate([main, rest], axis=1)[:30] * loss_scale
    channel_grads = sums[:15].reshape(3, width) * loss_scale
    return (field_grad.reshape(field.shape), kernel_grad, channel_grads)


def solution(mesh):
    spread = P("dp", "tm", "height", None, None)
    return jax.shard_map(
        per_device,
        mesh=mesh,
        in_specs=(spread, spread, P(), P(), P()),
        out_specs=(spread, P(("tm", "height"), "dp"), P()),
        check_vma=False,
    )
```
